32 devices in a mesh: tile: 4 (over x, core), dev: 8 (over z, y).
Axes of the slice: x: 2, y: 2, z: 4, core: 2. Of those that a mesh axis runs over, the one named last changes fastest.
Arguments:
- features: bfloat16 [256, 64, 128], P(('tile', 'dev')), may hold values from -6 to 6
- morton_pos: int32 [256], P(('tile', 'dev')), may hold values from 0 to 63, as said below
- neighbours: int32 [256, 27], P(('tile', 'dev')), may hold values from 0 to 24, as said below
- rim: int32 [128], P(('tile', 'dev')), may hold values from 0 to 7, as said below
- cotangent: bfloat16 [256, 64, 128], P(('tile', 'dev')), may hold values from -6 to 6
- weight_one: bfloat16 [3456, 128], replicated, may hold values from -0.109375 to 0.109375
- weight_two: bfloat16 [3456, 128], replicated, may hold values from -0.109375 to 0.109375
Outputs:
- output: bfloat16 [256, 64, 128], P(('tile', 'dev'))
- input_grad: bfloat16 [256, 64, 128], P(('tile', 'dev'))
- grad_one: float32 [3456, 128], replicated
- grad_two: float32 [3456, 128], replicated
The draws below stay inside these ranges and needn't reach their ends.
Inputs may be any that keep to these rules, and one draw needn't show every extreme that they name: `morton_pos`: within each super-tile the positions form a permutation of its 64 Morton rows; the 8 scan rows of one device go to at most 2 rows of any one device (position // 8), a bound reached in every draw. `neighbours`: lists come from block coordinates of a sparse map, each device owning a box of 6 x 6 x 2 block cells, tile stepping along x and dev along y: block a's neighbour at offset o is b exactly when b's neighbour at offset 26 - o is a; every block that a neighbouring device reads is in that device's rim list; the four corner columns of every box are empty, so no block reads a device diagonal to its own. `rim`: 4 different blocks of the device.
All inputs are finite; a program needn't handle non-finite values.
Results may differ from the reference program's by a relative error of at most 0.0033.
Values may be sent and summed in bfloat16 or wider, within the bound.
No kernel may reach another device: no remote copies, remote signals or barrier semaphores. Data moves between devices by JAX's collectives and lax.ppermute only.
A program may use at most 128 MiB of HBM per device.

```python
import math
import jax
import jax.numpy as jnp
import numpy as np
from jax import lax

CH = 128
EDGE = 4
VOX = 64
KCOLS = 3456
BLK = 8
RIM = 4
BOX_XY = 6
BOX_Z = 2
CAP = 2
BLOCKS = 256
N_TILE = 4
N_DEV = 8


def layout(key):
    cells = BOX_XY * BOX_XY * BOX_Z
    index = np.arange(cells)
    cell_x = index // (BOX_XY * BOX_Z)
    cell_y = index // BOX_Z % BOX_XY
    edge_x = (cell_x == 0) | (cell_x == BOX_XY - 1)
    edge_y = (cell_y == 0) | (cell_y == BOX_XY - 1)
    on_face = (edge_x | edge_y) & ~(edge_x & edge_y)
    inside = ~(edge_x | edge_y)
    face_cells = jnp.asarray(index[on_face], jnp.int32)
    inner_cells = jnp.asarray(index[inside], jnp.int32)
    devices = N_TILE * N_DEV
    device_keys = jax.random.split(jax.random.fold_in(key, 11), devices)

    def place(device_key):
        keys = jax.random.split(device_key, 4)
        chosen_face = jax.random.permutation(keys[0], face_cells)[:RIM]
        chosen_inner = jax.random.permutation(keys[1], inner_cells)[:BLK - RIM]
        chosen = jnp.concatenate([chosen_face, chosen_inner])
        order = jax.random.permutation(keys[2], BLK)
        cell_of_slot = chosen[order]
        slot_of_chosen = jnp.zeros((BLK,), jnp.int32).at[order].set(jnp.arange(BLK, dtype=jnp.int32))
        rim_order = jax.random.permutation(keys[3], RIM)
        rim_slots = slot_of_chosen[rim_order]
        rim_of_face = jnp.zeros((RIM,), jnp.int32).at[rim_order].set(jnp.arange(RIM, dtype=jnp.int32))
        slot_grid = jnp.full((cells,), -1, jnp.int32).at[cell_of_slot].set(jnp.arange(BLK, dtype=jnp.int32))
        rim_grid = jnp.full((cells,), -1, jnp.int32).at[chosen_face].set(rim_of_face)
        return (cell_of_slot, rim_slots, slot_grid, rim_grid)
    cell_of_slot, rim_slots, slot_grid, rim_grid = jax.vmap(place)(device_keys)
    offsets = np.arange(27)
    off_x = jnp.asarray(offsets // 9 - 1, jnp.int32)[None, None, :]
    off_y = jnp.asarray(offsets // 3 % 3 - 1, jnp.int32)[None, None, :]
    off_z = jnp.asarray(offsets % 3 - 1, jnp.int32)[None, None, :]
    device = jnp.arange(devices, dtype=jnp.int32)[:, None, None]
    tile_of = device // N_DEV
    dev_of = device % N_DEV
    cell = cell_of_slot[:, :, None]
    near_x = cell // (BOX_XY * BOX_Z) + off_x
    near_y = cell // BOX_Z % BOX_XY + off_y
    near_z = cell % BOX_Z + off_z
    step_x = jnp.where(near_x < 0, -1, jnp.where(near_x >= BOX_XY, 1, 0))
    step_y = jnp.where(near_y < 0, -1, jnp.where(near_y >= BOX_XY, 1, 0))
    local_x = near_x - step_x * BOX_XY
    local_y = near_y - step_y * BOX_XY
    tile_new = tile_of + step_x
    dev_new = dev_of + step_y
    valid = (near_z >= 0) & (near_z < BOX_Z) & (tile_new >= 0) & (tile_new < N_TILE) & (dev_new >= 0) & (dev_new < N_DEV) & ((step_x == 0) | (step_y == 0))
    other = jnp.clip(tile_new, 0, N_TILE - 1) * N_DEV + jnp.clip(dev_new, 0, N_DEV - 1)
    other_cell = (local_x * BOX_XY + local_y) * BOX_Z + jnp.clip(near_z, 0, BOX_Z - 1)
    slot_there = slot_grid[other, other_cell]
    rim_there = rim_grid[other, other_cell]
    sides = jnp.where(step_x == -1, 0, jnp.where(step_x == 1, 1, jnp.where(step_y == -1, 2, 3)))
    is_local = (step_x == 0) & (step_y == 0)
    value = jnp.where(is_local, slot_there, BLK + sides * RIM + rim_there)
    value = jnp.where(valid & (slot_there >= 0), value, BLK + 4 * RIM)
    neighbours = value.reshape(devices * BLK, 27).astype(jnp.int32)
    tile_keys = jax.random.split(jax.random.fold_in(key, 23), N_TILE)

    def regroup(tile_key):
        keys = jax.random.split(tile_key, 4)
        spare = jnp.repeat(jnp.arange(1, N_DEV, dtype=jnp.int32), CAP)
        picked = jax.random.permutation(keys[0], spare)[:BLK - CAP]
        peers = jnp.arange(N_DEV, dtype=jnp.int32)
        counts = jnp.sum((picked[:, None] == peers[None, :]).astype(jnp.int32), axis=0)
        counts = counts + jnp.where(peers == 0, CAP, 0)
        shuffle = jax.random.permutation(keys[1], N_DEV)
        matrix = counts[(shuffle[None, :] - peers[:, None]) % N_DEV]
        offset = jnp.cumsum(matrix, axis=0) - matrix
        row_keys = jax.random.split(keys[2], N_DEV)
        dest_keys = jax.random.split(keys[3], N_DEV)

        def arrange_one(dest_key):
            return jax.random.permutation(dest_key, BLK)
        arrange = jax.vmap(arrange_one)(dest_keys)

        def source(src, row_key):
            counts_here = matrix[src]
            dest = jnp.repeat(peers, counts_here, total_repeat_length=BLK)
            start = jnp.cumsum(counts_here) - counts_here
            spot = jnp.arange(BLK, dtype=jnp.int32) - start[dest] + offset[src, dest]
            position = dest * BLK + arrange[dest, spot]
            return position[jax.random.permutation(row_key, BLK)]
        return jax.vmap(source)(peers, row_keys).reshape(-1)
    morton = jax.vmap(regroup)(tile_keys).reshape(-1).astype(jnp.int32)
    return (morton, neighbours, rim_slots.reshape(-1).astype(jnp.int32))


def draw_morton_pos(key, part):
    return layout(key)[0]


def draw_neighbours(key, part):
    return layout(key)[1]


def draw_rim(key, part):
    return layout(key)[2]


def level_of(rng, extent, cuts, low, top_value):
    factor_of, own = 1.0, jax.random.fold_in(rng, 6)
    for axis_at, parts in cuts:
        steps = jnp.exp(jax.random.uniform(jax.random.fold_in(own, axis_at), (parts,), jnp.float32, low / len(cuts), top_value / len(cuts)))
        factor_of = factor_of * jnp.repeat(steps, extent[axis_at] // parts).reshape([-1 if axis == axis_at else 1 for axis in range(len(extent))])
    return factor_of


def bell_draw(rng, dims, deviation, reach, cuts=(), held_as=jnp.bfloat16):
    values = deviation * jax.random.normal(rng, dims, jnp.float32)
    if cuts:
        values = values * level_of(rng, dims, cuts, -0.22, 0.18)
    return jnp.clip(values, -reach, reach).astype(held_as)


def setup_inputs(seed: int = 0) -> dict:
    key_of = jax.random.split(jax.random.key(seed), 8)
    features = bell_draw(key_of[0], (BLOCKS, VOX, CH), 1.0, 6.0, ((0, 32),))
    morton_pos = draw_morton_pos(jax.random.fold_in(key_of[7], 71), 0)
    neighbours = draw_neighbours(jax.random.fold_in(key_of[7], 71), 0)
    rim = draw_rim(jax.random.fold_in(key_of[7], 71), 0)
    cotangent = bell_draw(key_of[4], (BLOCKS, VOX, CH), 1.0, 6.0, ((0, 32),))
    weight_one = bell_draw(key_of[5], (KCOLS, CH), KCOLS ** -0.5, 0.109375)
    weight_two = bell_draw(key_of[6], (KCOLS, CH), KCOLS ** -0.5, 0.109375)
    return dict(features=features, morton_pos=morton_pos, neighbours=neighbours, rim=rim, cotangent=cotangent, weight_one=weight_one, weight_two=weight_two)


def padded_cube(blocks):
    count = blocks.shape[0]
    channels = blocks.shape[-1]
    cube = blocks.reshape(count, 3, 3, 3, EDGE, EDGE, EDGE, channels)
    for axis_pass in range(3):
        cube = jnp.concatenate([cube[:, 0][:, :, :, EDGE - 1:], cube[:, 1], cube[:, 2][:, :, :, :1]], axis=3)
    return cube

def patch_columns(blocks):
    count = blocks.shape[0]
    channels = blocks.shape[-1]
    cube = padded_cube(blocks)
    pieces = [cube[:, offset_x:offset_x + EDGE, offset_y:offset_y + EDGE, offset_z:offset_z + EDGE] for offset_x in range(3) for offset_y in range(3) for offset_z in range(3)]
    return jnp.concatenate(pieces, axis=-1).reshape(count * EDGE ** 3, 27 * channels)

def global_rows(neighbours, rim):
    device = (jnp.arange(BLOCKS, dtype=jnp.int32) // BLK)[:, None]
    tile_of = device // N_DEV
    dev_of = device % N_DEV
    slot = jnp.clip(neighbours - BLK, 0, 4 * RIM - 1)
    sides = slot // RIM
    place = slot % RIM
    tile_new = tile_of + jnp.where(sides == 0, -1, jnp.where(sides == 1, 1, 0))
    dev_new = dev_of + jnp.where(sides == 2, -1, jnp.where(sides == 3, 1, 0))
    valid = (tile_new >= 0) & (tile_new < N_TILE) & (dev_new >= 0) & (dev_new < N_DEV)
    other = jnp.clip(tile_new, 0, N_TILE - 1) * N_DEV + jnp.clip(dev_new, 0, N_DEV - 1)
    remote = other * BLK + rim[other * RIM + place]
    result = jnp.where(neighbours < BLK, device * BLK + neighbours, jnp.where((neighbours < BLK + 4 * RIM) & valid, remote, BLOCKS))
    return result.astype(jnp.int32)

def reference(features, morton_pos, neighbours, rim, cotangent, weight_one, weight_two):
    per_tile = N_DEV * BLK
    scan_rows = jnp.arange(BLOCKS, dtype=jnp.int32)
    target = (scan_rows // per_tile * per_tile + morton_pos).astype(jnp.int32)
    morton = jnp.zeros_like(features).at[target].set(features)
    table_rows = global_rows(neighbours, rim).reshape(-1, BLK, 27)

    def forward(table, weight):
        padded = jnp.concatenate([table, jnp.zeros((1, VOX, CH), table.dtype)])

        def one_group(rows):
            return jnp.dot(patch_columns(padded[rows]), weight, preferred_element_type=jnp.float32)
        return lax.map(one_group, table_rows).reshape(BLOCKS, VOX, CH)

    def backward(table, grad, weight):
        padded = jnp.concatenate([table, jnp.zeros((1, VOX, CH), table.dtype)])
        grads = grad.reshape(-1, BLK * VOX, CH)

        def step(carry, inputs):
            total, wgrad = carry
            rows, local_grad = inputs
            blocks = padded[rows]
            columns = patch_columns(blocks)
            wgrad = wgrad + lax.dot_general(columns, local_grad, (((0,), (0,)), ((), ())), preferred_element_type=jnp.float32)
            back_cols = lax.dot_general(local_grad, weight, (((1,), (1,)), ((), ())), preferred_element_type=jnp.float32)
            primal = jnp.zeros(blocks.shape, jnp.float32)
            unused, pullback = jax.vjp(patch_columns, primal)
            back_blocks = pullback(back_cols)[0]
            total = total.at[rows.reshape(-1)].add(back_blocks.reshape(-1, VOX, CH))
            return ((total, wgrad), None)
        start = (jnp.zeros((BLOCKS + 1, VOX, CH), jnp.float32), jnp.zeros((27 * CH, CH), jnp.float32))
        (total, wgrad), unused = lax.scan(step, start, (table_rows, grads))
        return (total[:BLOCKS], wgrad)
    pre_one = forward(morton, weight_one)
    hidden = jax.nn.silu(pre_one).astype(jnp.bfloat16)
    pre_two = forward(hidden, weight_two)
    output = (morton.astype(jnp.float32) + pre_two).astype(jnp.bfloat16)
    hidden_grad, grad_two = backward(hidden, cotangent, weight_two)
    gate = jax.nn.sigmoid(pre_one)
    pre_grad = (hidden_grad * gate * (1.0 + pre_one * (1.0 - gate))).astype(jnp.bfloat16)
    morton_part, grad_one = backward(morton, pre_grad, weight_one)
    morton_grad = (morton_part + cotangent.astype(jnp.float32)).astype(jnp.bfloat16)
    input_grad = morton_grad[target]
    scale = 1.0 / math.sqrt(BLOCKS * VOX)
    return (output, input_grad, grad_one * scale, grad_two * scale)
```

```python
import functools
import math

import jax
import jax.numpy as jnp
from jax import lax
from jax.experimental import pallas as pl
from jax.experimental.pallas import tpu as pltpu
from jax.sharding import PartitionSpec as P

EDGE = 4
OFFSETS = 27
LABEL_ROWS = 16
BF16 = jnp.bfloat16
F32 = jnp.float32


def cube_plan():
    cell = {}
    for i in range(EDGE):
        for j in range(EDGE):
            for k in range(EDGE):
                cell[(i + 1, j + 1, k + 1)] = (i * EDGE + j) * EDGE + k
    copies = []
    free = EDGE**3
    for offset in range(OFFSETS):
        steps = (offset // 9 - 1, offset // 3 % 3 - 1, offset % 3 - 1)
        if steps == (0, 0, 0):
            continue
        ranges = [
            {-1: [(0, EDGE - 1)], 0: [(u + 1, u) for u in range(EDGE)], 1: [(EDGE + 1, 0)]}[step]
            for step in steps
        ]
        sources = []
        for x, i in ranges[0]:
            for y, j in ranges[1]:
                for z, k in ranges[2]:
                    cell[(x, y, z)] = free + len(sources)
                    sources.append((i * EDGE + j) * EDGE + k)
        at = 0
        while at < len(sources):
            count, stride = 1, 1
            if at + 1 < len(sources):
                stride = sources[at + 1] - sources[at]
                while (
                    at + count < len(sources)
                    and sources[at + count] - sources[at + count - 1] == stride
                ):
                    count += 1
            if count == 1:
                stride = 1
            copies.append((offset, sources[at], count, stride, free + at))
            at += count
        free += len(sources)
    return cell, copies, free


CELL, COPIES, CELLS = cube_plan()


def cell_runs(offset, flip):
    steps = (offset // 9, offset // 3 % 3, offset % 3)
    if flip:
        steps = tuple(2 - step for step in steps)
    runs = []
    for i in range(EDGE):
        for j in range(EDGE):
            for k in range(EDGE):
                at = CELL[(i + steps[0], j + steps[1], k + steps[2])]
                if runs and runs[-1][0] + runs[-1][1] == at:
                    runs[-1][1] += 1
                else:
                    runs.append([at, 1])
    return runs


def fill_table(table, own, sides, meta, at=0):
    blocks = own.shape[0]
    rims = sides[0].shape[0] if at is None else sides[0].shape[1]
    tile_odd = meta[0]
    dev_odd = meta[1]
    firsts = (
        blocks + rims * (1 - tile_odd),
        blocks + rims * tile_odd,
        blocks + rims * (3 - dev_odd),
        blocks + rims * (2 + dev_odd),
    )
    table[0:blocks] = own[...].astype(F32)
    for first, side in zip(firsts, sides):
        table[pl.ds(first, rims)] = (side[...] if at is None else side[at]).astype(F32)
    table[blocks + 4 * rims] = jnp.zeros(table.shape[1:], F32)


def fill_cells(cells, table, near, blocks):
    voxels = table.shape[1]
    for a in range(blocks):
        cells[pl.ds(a, voxels, stride=blocks), :] = table[a]
        for offset, first, count, stride, at in COPIES:
            e = near[a, offset]
            source = pl.ds(first, count) if stride == 1 else pl.ds(first, count, stride=stride)
            if count == 1:
                cells[pl.ds(at * blocks + a, 1), :] = table[e, source, :]
            else:
                cells[pl.ds(at * blocks + a, count, stride=blocks), :] = table[e, source, :]


def fill_columns(columns, cells, blocks, flip):
    channels = cells.shape[1]
    for offset in range(OFFSETS):
        parts = [
            cells[pl.ds(at * blocks, count * blocks), :] for at, count in cell_runs(offset, flip)
        ]
        columns[:, offset * channels : (offset + 1) * channels] = jnp.concatenate(
            parts, axis=0
        ).astype(BF16)


def transpose_blocks(target, source):
    channels = source.shape[1]
    for offset in range(OFFSETS):
        rows = slice(offset * channels, (offset + 1) * channels)
        target[rows, :] = source[rows, :].T


def pack_kernel(morton_pos, rim, features, cotangent, outgoing, rim_rows, flat_index):
    blocks, voxels, channels = features.shape
    peers, rows, _ = outgoing.shape
    capacity = (rows - LABEL_ROWS) // voxels
    outgoing[...] = jnp.zeros(outgoing.shape, BF16)
    for p in range(peers):
        outgoing[p, capacity * voxels :, :] = jnp.full((LABEL_ROWS, channels), blocks, BF16)
    lane = lax.broadcasted_iota(jnp.int32, (LABEL_ROWS, channels), 1)
    devs = [lax.div(morton_pos[r], blocks) for r in range(blocks)]
    for r in range(blocks):
        slot = morton_pos[r] - devs[r] * blocks
        place = jnp.int32(0)
        for earlier in range(r):
            place = place + (devs[earlier] == devs[r]).astype(jnp.int32)
        flat_index[r] = devs[r] * capacity + place
        outgoing[devs[r], pl.ds(pl.multiple_of(place * voxels, voxels), voxels), :] = features[r]
        held = outgoing[devs[r], capacity * voxels :, :].astype(F32)
        outgoing[devs[r], capacity * voxels :, :] = jnp.where(
            lane == place, slot.astype(F32), held
        ).astype(BF16)
    for h in range(rim_rows.shape[0]):
        rim_rows[h] = cotangent[rim[h]]


def unpack_kernel(slots, rim, arrived, morton, rim_rows):
    blocks, voxels, channels = morton.shape
    peers, rows, _ = arrived.shape
    capacity = (rows - LABEL_ROWS) // voxels
    for p in range(peers):
        for c in range(capacity):
            slot = slots[p * capacity + c]

            @pl.when(slot < blocks)
            def _():
                morton[slot] = arrived[p, c * voxels : (c + 1) * voxels, :]

    for h in range(rim_rows.shape[0]):
        rim_rows[h] = morton[rim[h]]


def first_kernel(
    near, meta, cotangent, side_a, side_b, side_c, side_d, weight_one, weight_two,
    columns, hidden_grad, flipped_one, table, cells, flipped_two,
):
    blocks = cotangent.shape[0]
    fill_table(table, cotangent, (side_a, side_b, side_c, side_d), meta, None)
    fill_cells(cells, table, near, blocks)
    fill_columns(columns, cells, blocks, True)
    transpose_blocks(flipped_two, weight_two)
    hidden_grad[...] = jnp.dot(columns[...], flipped_two[...], preferred_element_type=F32)
    transpose_blocks(flipped_one, weight_one)


def middle_kernel(
    near, meta, rim, morton, side_a, side_b, side_c, side_d, weight_one, grad_columns, hidden_grad,
    hidden, pre_grad, rim_rows, keep_two, send_two, keep_one, send_one,
    table, cells, columns, hidden_va, pre_grad_va, halves,
):
    blocks, voxels, channels = morton.shape
    half = channels // 2
    core = meta[0]
    fill_table(table, morton, (side_a, side_b, side_c, side_d), meta, None)
    fill_cells(cells, table, near, blocks)
    fill_columns(columns, cells, blocks, False)
    pre_one = jnp.dot(columns[...], weight_one[...], preferred_element_type=F32)
    gate = jax.nn.sigmoid(pre_one)
    hidden_flat = (pre_one * gate).astype(BF16)
    pre_grad_flat = (hidden_grad[...] * gate * (1.0 + pre_one * (1.0 - gate))).astype(BF16)
    hidden_va[...] = hidden_flat.astype(F32)
    pre_grad_va[...] = pre_grad_flat.astype(F32)
    for a in range(blocks):
        hidden[a] = hidden_va[pl.ds(a, voxels, stride=blocks), :].astype(BF16)
        pre_grad[a] = pre_grad_va[pl.ds(a, voxels, stride=blocks), :].astype(BF16)
    for h in range(rim_rows.shape[1]):
        rim_rows[0, h] = hidden[rim[h]]
        rim_rows[1, h] = pre_grad[rim[h]]
    turned = hidden_flat.T
    for offset in range(OFFSETS):
        part = jnp.dot(
            turned,
            grad_columns[:, offset * channels : (offset + 1) * channels],
            preferred_element_type=F32,
        )
        halves[core, offset] = part[:half]
        halves[1 - core, offset] = part[half:]
    keep_two[0:OFFSETS] = halves[0]
    send_two[0:OFFSETS] = halves[1]
    turned = pre_grad_flat.T
    for offset in range(OFFSETS):
        part = jnp.dot(
            turned,
            columns[:, offset * channels : (offset + 1) * channels],
            preferred_element_type=F32,
        ).T
        halves[core, offset] = part[:half]
        halves[1 - core, offset] = part[half:]
    keep_one[0:OFFSETS] = halves[0]
    send_one[0:OFFSETS] = halves[1]
    for ref in (keep_two, send_two, keep_one, send_one):
        ref[OFFSETS] = jnp.zeros(ref.shape[1:], F32)


def last_kernel(
    near, meta, slots, hidden, pre_grad, morton, cotangent, side_a, side_b, side_c, side_d,
    weight_two, flipped_one, output, returning, table, cells, columns, result, natural,
):
    blocks, voxels, channels = morton.shape
    peers, rows, _ = returning.shape
    capacity = rows // voxels
    sides = (side_a, side_b, side_c, side_d)
    fill_table(table, hidden, sides, meta, 0)
    fill_cells(cells, table, near, blocks)
    fill_columns(columns, cells, blocks, False)
    result[...] = jnp.dot(columns[...], weight_two[...], preferred_element_type=F32)
    for a in range(blocks):
        output[a] = (
            morton[a].astype(F32) + result[pl.ds(a, voxels, stride=blocks), :]
        ).astype(BF16)
    fill_table(table, pre_grad, sides, meta, 1)
    fill_cells(cells, table, near, blocks)
    fill_columns(columns, cells, blocks, True)
    result[...] = jnp.dot(columns[...], flipped_one[...], preferred_element_type=F32)
    for a in range(blocks):
        natural[a] = (
            result[pl.ds(a, voxels, stride=blocks), :] + cotangent[a].astype(F32)
        ).astype(BF16)
    natural[blocks] = jnp.zeros((voxels, channels), BF16)
    for p in range(peers):
        for c in range(capacity):
            returning[p, c * voxels : (c + 1) * voxels, :] = natural[slots[p * capacity + c]]


def restore_kernel(flat_index, coming_back, input_grad):
    blocks, voxels, channels = input_grad.shape
    for r in range(blocks):
        input_grad[r] = coming_back[flat_index[r]]


def core_sum_kernel(meta, keep, received, total, out_a, out_b, out_c, held):
    held[...] = keep[...] + received[...]
    rows = total.shape[1]
    mine = meta[2] + 2 * meta[3]

    def part(index):
        return held[:, pl.ds(pl.multiple_of(index * rows, rows), rows), :]

    total[...] = part(mine)
    out_a[...] = part(mine ^ 1).astype(BF16)
    out_b[...] = part(mine ^ 2).astype(BF16)
    out_c[...] = part(mine ^ 3).astype(BF16)


def quad_sum_kernel(meta, total, in_a, in_b, in_c, keep, send, held):
    held[...] = (
        total[...] + in_a[...].astype(F32) + in_b[...].astype(F32) + in_c[...].astype(F32)
    )
    count = keep.shape[0]
    keep[...] = held[pl.ds(meta[4] * count, count)]
    send[...] = held[pl.ds((1 - meta[4]) * count, count)].astype(send.dtype)


def add_kernel(left, right, total):
    total[...] = (left[...].astype(F32) + right[...].astype(F32)).astype(total.dtype)


def join_kernel(meta, mine, other, joined):
    count = mine.shape[0]
    joined[pl.ds(meta[4] * count, count)] = mine[...]
    joined[pl.ds((1 - meta[4]) * count, count)] = other[...]


def quad_join_kernel(meta, mine, in_a, in_b, in_c, joined):
    rows = mine.shape[1]
    index = meta[2] + 2 * meta[3]
    for m, ref in enumerate((mine, in_a, in_b, in_c)):
        joined[:, pl.ds(pl.multiple_of((index ^ m) * rows, rows), rows), :] = ref[...]


def finish_kernel(scale, meta, mine, other, grad):
    rows = mine.shape[1]
    channels = mine.shape[2]
    first = pl.multiple_of(meta[0] * rows, rows)
    second = pl.multiple_of((1 - meta[0]) * rows, rows)
    for offset in range(OFFSETS):
        grad[pl.ds(offset * channels + first, rows), :] = mine[offset].astype(F32) * scale
        grad[pl.ds(offset * channels + second, rows), :] = other[offset].astype(F32) * scale


SMEM = pl.BlockSpec(memory_space=pltpu.SMEM)
VMEM = pl.BlockSpec(memory_space=pltpu.VMEM)


def call(kernel, scalars, arrays, outs, scratch=(), smem_outs=(), flops=0, name=None):
    shapes = [jax.ShapeDtypeStruct(shape, dtype) for shape, dtype in outs]
    shapes += [jax.ShapeDtypeStruct(shape, jnp.int32) for shape in smem_outs]
    moved = sum(x.size * x.dtype.itemsize for x in arrays)
    moved += sum(math.prod(s.shape) * s.dtype.itemsize for s in shapes)
    return pl.pallas_call(
        kernel,
        out_shape=shapes,
        in_specs=[SMEM] * len(scalars) + [VMEM] * len(arrays),
        out_specs=[VMEM] * len(outs) + [SMEM] * len(smem_outs),
        scratch_shapes=[pltpu.VMEM(shape, dtype) for shape, dtype in scratch],
        compiler_params=pltpu.CompilerParams(vmem_limit_bytes=48 * 2**20),
        cost_estimate=pl.CostEstimate(flops=flops, bytes_accessed=moved, transcendentals=0),
        name=name,
    )(*scalars, *arrays)


def halo(rows):
    sides = []
    for axis in ("tile", "dev"):
        count = lax.axis_size(axis)
        even = [(i, i ^ 1) for i in range(count)]
        odd = []
        for i in range(1, count - 1, 2):
            odd += [(i, i + 1), (i + 1, i)]
        sides += [lax.ppermute(rows, axis, even), lax.ppermute(rows, axis, odd)]
    return sides


def swap(rows, tile_bit, dev_bit):
    tiles, devs = lax.axis_size("tile"), lax.axis_size("dev")
    pairs = [
        (t * devs + d, (t ^ tile_bit) * devs + (d ^ dev_bit))
        for t in range(tiles)
        for d in range(devs)
    ]
    return lax.ppermute(rows, ("tile", "dev"), pairs)


def reduce_all(meta, keep, send, scale):
    tiles, devs = lax.axis_size("tile"), lax.axis_size("dev")
    count, rows, channels = keep.shape
    quarter = rows // 4
    small = (count, quarter, channels)
    received = swap(send, 1, 0)
    total, out_a, out_b, out_c = call(
        core_sum_kernel, [meta], [keep, received],
        [(small, F32), (small, BF16), (small, BF16), (small, BF16)],
        [(keep.shape, F32)], name="core_sum",
    )
    in_a, in_b, in_c = swap(out_a, 2, 0), swap(out_b, 0, 1), swap(out_c, 2, 1)
    part = (count // 2, quarter, channels)
    keep, send = call(
        quad_sum_kernel, [meta], [total, in_a, in_b, in_c], [(part, F32), (part, F32)],
        [(small, F32)], name="quad_sum",
    )
    received = swap(send, 0, 2)
    rest = [(0, 1 << bit) for bit in range(2, devs.bit_length() - 1)]
    rest += [(1 << bit, 0) for bit in range(2, tiles.bit_length() - 1)]
    wire = BF16 if len(rest) == 1 else F32
    (mine,) = call(add_kernel, [], [keep, received], [(part, wire)], name="pair_sum")
    for step, (tile_bit, dev_bit) in enumerate(rest):
        other = swap(mine, tile_bit, dev_bit)
        kind = BF16 if step == len(rest) - 1 else wire
        (mine,) = call(add_kernel, [], [mine, other], [(part, kind)], name="far_sum")
    other = swap(mine, 0, 2)
    (mine,) = call(join_kernel, [meta], [mine, other], [(small, BF16)], name="pair_join")
    others = [swap(mine, 2, 0), swap(mine, 0, 1), swap(mine, 2, 1)]
    (mine,) = call(
        quad_join_kernel, [meta], [mine, *others], [((count, rows, channels), BF16)],
        name="quad_join",
    )
    other = swap(mine, 1, 0)
    (grad,) = call(
        functools.partial(finish_kernel, scale), [meta], [mine, other],
        [((OFFSETS * channels, channels), F32)], name="finish",
    )
    return grad


def per_device(features, morton_pos, neighbours, rim, cotangent, weight_one, weight_two):
    blocks, voxels, channels = features.shape
    rims = rim.shape[0]
    peers = lax.axis_size("dev")
    tiles = lax.axis_size("tile")
    capacity = 2 * ((blocks + peers - 1) // peers)
    t, d = lax.axis_index("tile"), lax.axis_index("dev")
    meta = jnp.stack([t & 1, d & 1, (t >> 1) & 1, d & 1, (d >> 1) & 1]).astype(jnp.int32)
    block = (blocks, voxels, channels)
    rows = blocks * voxels
    depth = OFFSETS * channels
    table = ((blocks + 4 * rims + 1, voxels, channels), F32)
    cells = ((CELLS * blocks, channels), F32)
    columns = ((rows, depth), BF16)
    flat = ((rows, channels), F32)
    rim_shape = (rims, voxels, channels)
    macs = rows * depth * channels

    outgoing, cot_rim, flat_index = call(
        pack_kernel, [morton_pos, rim], [features, cotangent],
        [((peers, capacity * voxels + LABEL_ROWS, channels), BF16), (rim_shape, BF16)],
        smem_outs=[(blocks,)], name="pack",
    )
    arrived = lax.all_to_all(outgoing, "dev", split_axis=0, concat_axis=0, tiled=True)
    cot_sides = halo(cot_rim)
    grad_columns, hidden_grad, flipped_one = call(
        first_kernel, [neighbours, meta], [cotangent, *cot_sides, weight_one, weight_two],
        [columns, flat, ((depth, channels), BF16)],
        [table, cells, ((depth, channels), BF16)], flops=2 * macs, name="hidden_grad",
    )
    slots = arrived[:, capacity * voxels, :capacity].astype(jnp.int32).reshape(-1)
    morton, morton_rim = call(
        unpack_kernel, [slots, rim], [arrived], [(block, BF16), (rim_shape, BF16)], name="unpack"
    )
    sides = halo(morton_rim)
    padded = (OFFSETS + 1, channels // 2, channels)
    hidden, pre_grad, rim_rows, keep_two, send_two, keep_one, send_one = call(
        middle_kernel, [neighbours, meta, rim],
        [morton, *sides, weight_one, grad_columns, hidden_grad],
        [(block, BF16), (block, BF16), ((2,) + rim_shape, BF16)] + [(padded, F32)] * 4,
        [table, cells, columns, flat, flat, ((2, OFFSETS, channels // 2, channels), F32)],
        flops=6 * macs, name="middle",
    )
    scale = 1.0 / math.sqrt(blocks * voxels * tiles * peers)
    grad_two = reduce_all(meta, keep_two, send_two, scale)
    grad_one = reduce_all(meta, keep_one, send_one, scale)
    sides = halo(rim_rows)
    output, returning = call(
        last_kernel, [neighbours, meta, slots],
        [hidden, pre_grad, morton, cotangent, *sides, weight_two, flipped_one],
        [(block, BF16), ((peers, capacity * voxels, channels), BF16)],
        [table, cells, columns, flat, ((blocks + 1, voxels, channels), BF16)],
        flops=4 * macs, name="last",
    )
    coming_back = lax.all_to_all(returning, "dev", split_axis=0, concat_axis=0, tiled=True)
    (input_grad,) = call(
        restore_kernel, [flat_index], [coming_back.reshape(peers * capacity, voxels, channels)],
        [(block, BF16)], name="restore",
    )
    return (output, input_grad, grad_one, grad_two)


def solution(mesh):
    placed = (
        P(("tile", "dev"), None, None),
        P(("tile", "dev")),
        P(("tile", "dev"), None),
        P(("tile", "dev")),
        P(("tile", "dev"), None, None),
        P(),
        P(),
    )
    return jax.shard_map(
        per_device,
        mesh=mesh,
        in_specs=placed,
        out_specs=(P(("tile", "dev"), None, None), P(("tile", "dev"), None, None), P(), P()),
        check_vma=False,
    )
```

```python
import functools
import math

import jax
import jax.numpy as jnp
from jax import lax
from jax.experimental import pallas as pl
from jax.experimental.pallas import tpu as pltpu
from jax.sharding import PartitionSpec as P

EDGE = 4
OFFSETS = 27
LABEL_ROWS = 16
WAIT = 1_500_000_000
BF16 = jnp.bfloat16
F32 = jnp.float32


def cube_plan():
    cell = {}
    for i in range(EDGE):
        for j in range(EDGE):
            for k in range(EDGE):
                cell[(i + 1, j + 1, k + 1)] = (i * EDGE + j) * EDGE + k
    copies = []
    free = EDGE**3
    for offset in range(OFFSETS):
        steps = (offset // 9 - 1, offset // 3 % 3 - 1, offset % 3 - 1)
        if steps == (0, 0, 0):
            continue
        ranges = [
            {-1: [(0, EDGE - 1)], 0: [(u + 1, u) for u in range(EDGE)], 1: [(EDGE + 1, 0)]}[step]
            for step in steps
        ]
        sources = []
        for x, i in ranges[0]:
            for y, j in ranges[1]:
                for z, k in ranges[2]:
                    cell[(x, y, z)] = free + len(sources)
                    sources.append((i * EDGE + j) * EDGE + k)
        at = 0
        while at < len(sources):
            count, stride = 1, 1
            if at + 1 < len(sources):
                stride = sources[at + 1] - sources[at]
                while (
                    at + count < len(sources)
                    and sources[at + count] - sources[at + count - 1] == stride
                ):
                    count += 1
            if count == 1:
                stride = 1
            copies.append((offset, sources[at], count, stride, free + at))
            at += count
        free += len(sources)
    return cell, copies, free


CELL, COPIES, CELLS = cube_plan()


def cell_runs(offset, flip):
    steps = (offset // 9, offset // 3 % 3, offset % 3)
    if flip:
        steps = tuple(2 - step for step in steps)
    runs = []
    for i in range(EDGE):
        for j in range(EDGE):
            for k in range(EDGE):
                at = CELL[(i + steps[0], j + steps[1], k + steps[2])]
                if runs and runs[-1][0] + runs[-1][1] == at:
                    runs[-1][1] += 1
                else:
                    runs.append([at, 1])
    return runs


def parity(axis, bit=0):
    return (lax.axis_index(axis) >> bit) & 1


def fill_table(table, own, sides, at=None):
    blocks = own.shape[0]
    rims = sides[0].shape[0] if at is None else sides[0].shape[1]
    tile_odd = parity("tile")
    dev_odd = parity("dev")
    firsts = (
        blocks + rims * (1 - tile_odd),
        blocks + rims * tile_odd,
        blocks + rims * (3 - dev_odd),
        blocks + rims * (2 + dev_odd),
    )
    table[0:blocks] = own[...].astype(F32)
    for first, side in zip(firsts, sides):
        table[pl.ds(first, rims)] = (side[...] if at is None else side[at]).astype(F32)
    table[blocks + 4 * rims] = jnp.zeros(table.shape[1:], F32)


def fill_cells(cells, table, near, blocks):
    voxels = table.shape[1]
    for a in range(blocks):
        cells[pl.ds(a, voxels, stride=blocks), :] = table[a]
        for offset, first, count, stride, at in COPIES:
            e = near[a, offset]
            source = pl.ds(first, count) if stride == 1 else pl.ds(first, count, stride=stride)
            if count == 1:
                cells[pl.ds(at * blocks + a, 1), :] = table[e, source, :]
            else:
                cells[pl.ds(at * blocks + a, count, stride=blocks), :] = table[e, source, :]


def fill_columns(columns, cells, blocks, flip):
    channels = cells.shape[1]
    for offset in range(OFFSETS):
        parts = [
            cells[pl.ds(at * blocks, count * blocks), :] for at, count in cell_runs(offset, flip)
        ]
        columns[:, offset * channels : (offset + 1) * channels] = jnp.concatenate(
            parts, axis=0
        ).astype(BF16)


def flipped_dot(columns, weight):
    channels = weight.shape[1]
    total = jnp.zeros((columns.shape[0], channels), F32)
    for offset in range(OFFSETS):
        part = slice(offset * channels, (offset + 1) * channels)
        total = total + lax.dot_general(
            columns[:, part], weight[part, :], (((1,), (1,)), ((), ())), preferred_element_type=F32
        )
    return total


def fetch(sems, *pairs):
    copies = [
        pltpu.make_async_copy(source, target, sems.at[n])
        for n, (source, target) in enumerate(pairs)
    ]
    for copy in copies:
        copy.start()
    return copies


def places_of(morton_pos, blocks):
    devs = [lax.div(morton_pos[r], blocks) for r in range(blocks)]
    places = []
    for r in range(blocks):
        place = jnp.int32(0)
        for earlier in range(r):
            place = place + (devs[earlier] == devs[r]).astype(jnp.int32)
        places.append(place)
    return devs, places


def pack_kernel(
    morton_hbm, rim_hbm, features_hbm, cotangent_hbm,
    outgoing, rim_rows, rim_tiles, morton_pos, rim, features, cotangent, sems,
):
    blocks, voxels, channels = features.shape
    peers, rows, _ = outgoing.shape
    capacity = (rows - LABEL_ROWS) // voxels
    copies = fetch(
        sems, (morton_hbm, morton_pos), (features_hbm, features), (rim_hbm, rim),
        (cotangent_hbm, cotangent),
    )
    outgoing[...] = jnp.zeros(outgoing.shape, BF16)
    for p in range(peers):
        outgoing[p, capacity * voxels :, :] = jnp.full((LABEL_ROWS, channels), blocks, BF16)
    row = lax.broadcasted_iota(jnp.int32, (LABEL_ROWS, channels), 0)
    copies[0].wait()
    devs, places = places_of(morton_pos, blocks)
    copies[1].wait()
    for r in range(blocks):
        slot = morton_pos[r] - devs[r] * blocks
        place = places[r]
        outgoing[devs[r], pl.ds(pl.multiple_of(place * voxels, voxels), voxels), :] = features[r]
        held = outgoing[devs[r], capacity * voxels :, :].astype(F32)
        outgoing[devs[r], capacity * voxels :, :] = jnp.where(
            row == place, slot.astype(F32), held
        ).astype(BF16)
    copies[2].wait()
    copies[3].wait()
    for h in range(rim_rows.shape[0]):
        rim_rows[h] = cotangent[rim[h]]
        rim_tiles[h] = jnp.full(rim_tiles.shape[1:], rim[h].astype(F32), F32)


def tiles_of(rows):
    return rows.astype(F32).reshape(-1, 8, rows.shape[-1])


def unpack_kernel(arrived, rim_tiles, morton, rim_rows, labels):
    blocks, voxels, channels = morton.shape
    peers, rows, _ = arrived.shape
    capacity = (rows - LABEL_ROWS) // voxels
    held = [jnp.zeros((voxels // 8, 8, channels), F32) for _ in range(blocks)]
    for p in range(peers):
        for c in range(capacity):
            label = jnp.broadcast_to(
                arrived[p, capacity * voxels :, :].astype(F32)[c : c + 1], (8, channels)
            )
            labels[p * capacity + c] = label
            block = tiles_of(arrived[p, c * voxels : (c + 1) * voxels, :])
            for r in range(blocks):
                held[r] = jnp.where((label == r)[None], block, held[r])
    for r in range(blocks):
        morton[r] = held[r].reshape(voxels, channels).astype(BF16)
    for h in range(rim_rows.shape[0]):
        block = held[0]
        for r in range(1, blocks):
            block = jnp.where((rim_tiles[h] == r)[None], held[r], block)
        rim_rows[h] = block.reshape(voxels, channels).astype(BF16)


def first_kernel(
    near_hbm, cotangent_hbm, weight_hbm, side_a, side_b, side_c, side_d,
    columns, hidden_grad, near, cotangent, weight, table, cells, sems,
):
    blocks = cotangent.shape[0]
    copies = fetch(sems, (near_hbm, near), (cotangent_hbm, cotangent), (weight_hbm, weight))
    copies[1].wait()
    fill_table(table, cotangent, (side_a, side_b, side_c, side_d))
    copies[0].wait()
    fill_cells(cells, table, near, blocks)
    fill_columns(columns, cells, blocks, True)
    copies[2].wait()
    hidden_grad[...] = flipped_dot(columns, weight)


def store_halves(keep, send, offset, part, low):
    half = part.shape[0] // 2
    keep[offset] = jnp.where(low, part[:half], part[half:])
    send[offset] = jnp.where(low, part[half:], part[:half])


def middle_kernel(
    near_hbm, rim_hbm, weight_hbm, morton, side_a, side_b, side_c, side_d, grad_columns,
    hidden_grad, hidden, pre_grad, rim_rows, keep_two, send_two, keep_one, send_one,
    near, rim, weight, table, cells, columns, hidden_va, pre_grad_va, sems,
):
    blocks, voxels, channels = morton.shape
    copies = fetch(sems, (near_hbm, near), (rim_hbm, rim), (weight_hbm, weight))
    fill_table(table, morton, (side_a, side_b, side_c, side_d))
    copies[0].wait()
    fill_cells(cells, table, near, blocks)
    fill_columns(columns, cells, blocks, False)
    copies[1].wait()
    copies[2].wait()
    pre_one = jnp.dot(columns[...], weight[...], preferred_element_type=F32)
    gate = jax.nn.sigmoid(pre_one)
    hidden_flat = (pre_one * gate).astype(BF16)
    pre_grad_flat = (hidden_grad[...] * gate * (1.0 + pre_one * (1.0 - gate))).astype(BF16)
    hidden_va[...] = hidden_flat.astype(F32)
    pre_grad_va[...] = pre_grad_flat.astype(F32)
    for a in range(blocks):
        hidden[a] = hidden_va[pl.ds(a, voxels, stride=blocks), :].astype(BF16)
        pre_grad[a] = pre_grad_va[pl.ds(a, voxels, stride=blocks), :].astype(BF16)
    for h in range(rim_rows.shape[1]):
        rim_rows[0, h] = hidden[rim[h]]
        rim_rows[1, h] = pre_grad[rim[h]]
    low = jnp.full((channels // 2, channels), parity("tile"), jnp.int32) == 0
    turned = hidden_flat.T
    for offset in range(0, OFFSETS, 2):
        count = min(2, OFFSETS - offset)
        part = jnp.dot(
            turned,
            grad_columns[:, offset * channels : (offset + count) * channels],
            preferred_element_type=F32,
        )
        for u in range(count):
            store_halves(
                keep_two, send_two, offset + u, part[:, u * channels : (u + 1) * channels], low
            )
    turned = pre_grad_flat.T
    for offset in range(0, OFFSETS, 2):
        count = min(2, OFFSETS - offset)
        part = jnp.dot(
            turned,
            columns[:, offset * channels : (offset + count) * channels],
            preferred_element_type=F32,
        )
        for u in range(count):
            store_halves(
                keep_one, send_one, offset + u, part[:, u * channels : (u + 1) * channels].T, low
            )
    for ref in (keep_two, send_two, keep_one, send_one):
        ref[OFFSETS] = jnp.zeros(ref.shape[1:], F32)


def back_kernel(
    near_hbm, cotangent_hbm, weight_hbm, pre_grad, side_a, side_b, side_c, side_d, labels,
    returning, near, cotangent, weight, table, cells, columns, result, sems,
):
    blocks, voxels, channels = cotangent.shape
    peers, rows, _ = returning.shape
    capacity = rows // voxels
    copies = fetch(sems, (near_hbm, near), (cotangent_hbm, cotangent), (weight_hbm, weight))
    fill_table(table, pre_grad, (side_a, side_b, side_c, side_d), 1)
    copies[0].wait()
    fill_cells(cells, table, near, blocks)
    fill_columns(columns, cells, blocks, True)
    copies[1].wait()
    copies[2].wait()
    result[...] = flipped_dot(columns, weight)
    natural = [
        tiles_of(result[pl.ds(a, voxels, stride=blocks), :] + cotangent[a].astype(F32))
        for a in range(blocks)
    ]
    for p in range(peers):
        for c in range(capacity):
            label = labels[p * capacity + c]
            block = natural[0]
            for r in range(1, blocks):
                block = jnp.where((label == r)[None], natural[r], block)
            returning[p, c * voxels : (c + 1) * voxels, :] = block.reshape(
                voxels, channels
            ).astype(BF16)


def output_kernel(
    capacity, near_hbm, morton_hbm, weight_hbm, hidden, morton, side_a, side_b, side_c, side_d,
    output, flat_tiles, near, morton_pos, weight, table, cells, columns, result, sems,
):
    blocks, voxels, channels = morton.shape
    copies = fetch(sems, (near_hbm, near), (weight_hbm, weight), (morton_hbm, morton_pos))
    fill_table(table, hidden, (side_a, side_b, side_c, side_d), 0)
    copies[0].wait()
    fill_cells(cells, table, near, blocks)
    fill_columns(columns, cells, blocks, False)
    copies[1].wait()
    result[...] = jnp.dot(columns[...], weight[...], preferred_element_type=F32)
    for a in range(blocks):
        output[a] = (
            morton[a].astype(F32) + result[pl.ds(a, voxels, stride=blocks), :]
        ).astype(BF16)
    copies[2].wait()
    devs, places = places_of(morton_pos, blocks)
    for r in range(blocks):
        flat_tiles[r] = jnp.full(
            flat_tiles.shape[1:], (devs[r] * capacity + places[r]).astype(F32), F32
        )


def restore_kernel(coming_back, flat_tiles, input_grad):
    blocks, voxels, channels = input_grad.shape
    slots = coming_back.shape[0]
    held = [jnp.zeros((voxels // 8, 8, channels), F32) for _ in range(blocks)]
    for s in range(slots):
        block = tiles_of(coming_back[s])
        for r in range(blocks):
            held[r] = jnp.where((flat_tiles[r] == s)[None], block, held[r])
    for r in range(blocks):
        input_grad[r] = held[r].reshape(voxels, channels).astype(BF16)


def quad_index():
    return parity("tile", 1) + 2 * parity("dev")


def core_sum_kernel(keep, received, total, out_a, out_b, out_c):
    rows = total.shape[1]
    mine = quad_index()

    def part(index):
        at = pl.ds(pl.multiple_of(index * rows, rows), rows)
        return keep[:, at, :] + received[:, at, :]

    total[...] = part(mine)
    out_a[...] = part(mine ^ 1).astype(BF16)
    out_b[...] = part(mine ^ 2).astype(BF16)
    out_c[...] = part(mine ^ 3).astype(BF16)


def quad_sum_kernel(total, in_a, in_b, in_c, keep, send):
    count = keep.shape[0]
    side = parity("dev", 1)

    def part(index):
        at = pl.ds(index * count, count)
        return (
            total[at] + in_a[at].astype(F32) + in_b[at].astype(F32) + in_c[at].astype(F32)
        )

    keep[...] = part(side)
    send[...] = part(1 - side).astype(send.dtype)


def add_kernel(left, right, total):
    total[...] = (left[...].astype(F32) + right[...].astype(F32)).astype(total.dtype)


def join_kernel(mine, other, joined):
    count = mine.shape[0]
    side = parity("dev", 1)
    joined[pl.ds(side * count, count)] = mine[...]
    joined[pl.ds((1 - side) * count, count)] = other[...]


def quad_join_kernel(mine, in_a, in_b, in_c, joined):
    rows = mine.shape[1]
    index = quad_index()
    for m, ref in enumerate((mine, in_a, in_b, in_c)):
        joined[:, pl.ds(pl.multiple_of((index ^ m) * rows, rows), rows), :] = ref[...]


def finish_kernel(scale, mine, other, grad_hbm, grad, sems):
    rows, channels = mine.shape[1:]
    core = parity("tile")
    first = pl.multiple_of(core * rows, rows)
    second = pl.multiple_of((1 - core) * rows, rows)
    group = OFFSETS // 3
    copies = []
    for n in range(3):
        for offset in range(n * group, (n + 1) * group):
            grad[pl.ds(offset * channels + first, rows), :] = mine[offset].astype(F32) * scale
            grad[pl.ds(offset * channels + second, rows), :] = other[offset].astype(F32) * scale
        part = pl.ds(n * group * channels, group * channels)
        copies.append(pltpu.make_async_copy(grad.at[part], grad_hbm.at[part], sems.at[n]))
        copies[-1].start()
    for copy in copies:
        copy.wait()


HBM = pl.BlockSpec(memory_space=pltpu.HBM)
VMEM = pl.BlockSpec(memory_space=pltpu.VMEM)


def call(kernel, far, arrays, outs, scratch=(), far_outs=(), flops=0, name=None):
    shapes = [jax.ShapeDtypeStruct(shape, dtype) for shape, dtype in [*outs, *far_outs]]
    moved = sum(x.size * x.dtype.itemsize for x in [*far, *arrays])
    moved += sum(math.prod(s.shape) * s.dtype.itemsize for s in shapes)
    held = []
    for item in scratch:
        if isinstance(item, int):
            held.append(pltpu.SemaphoreType.DMA((item,)))
        else:
            held.append((pltpu.SMEM if item[1] == jnp.int32 else pltpu.VMEM)(*item))
    return pl.pallas_call(
        kernel,
        out_shape=shapes,
        in_specs=[HBM] * len(far) + [VMEM] * len(arrays),
        out_specs=[VMEM] * len(outs) + [HBM] * len(far_outs),
        scratch_shapes=held,
        compiler_params=pltpu.CompilerParams(vmem_limit_bytes=(63 if name == "pack" else 24) * 2**20),
        cost_estimate=pl.CostEstimate(flops=flops, bytes_accessed=moved, transcendentals=0),
        name=name,
    )(*far, *arrays)


def halo(rows):
    sides = []
    for axis in ("tile", "dev"):
        count = lax.axis_size(axis)
        even = [(i, i ^ 1) for i in range(count)]
        odd = []
        for i in range(1, count - 1, 2):
            odd += [(i, i + 1), (i + 1, i)]
        sides += [lax.ppermute(rows, axis, even), lax.ppermute(rows, axis, odd)]
    return sides


def swap(rows, tile_bit, dev_bit):
    tiles, devs = lax.axis_size("tile"), lax.axis_size("dev")
    pairs = [
        (t * devs + d, (t ^ tile_bit) * devs + (d ^ dev_bit))
        for t in range(tiles)
        for d in range(devs)
    ]
    return lax.ppermute(rows, ("tile", "dev"), pairs)


def reduce_all(keep, send, scale):
    tiles, devs = lax.axis_size("tile"), lax.axis_size("dev")
    count, rows, channels = keep.shape
    quarter = rows // 4
    small = (count, quarter, channels)
    received = swap(send, 1, 0)
    total, out_a, out_b, out_c = call(
        core_sum_kernel, [], [keep, received],
        [(small, F32), (small, BF16), (small, BF16), (small, BF16)], name="core_sum",
    )
    in_a, in_b, in_c = swap(out_a, 2, 0), swap(out_b, 0, 1), swap(out_c, 2, 1)
    part = (count // 2, quarter, channels)
    keep, send = call(
        quad_sum_kernel, [], [total, in_a, in_b, in_c], [(part, F32), (part, F32)],
        name="quad_sum",
    )
    received = swap(send, 0, 2)
    rest = [(0, 1 << bit) for bit in range(2, devs.bit_length() - 1)]
    rest += [(1 << bit, 0) for bit in range(2, tiles.bit_length() - 1)]
    wire = BF16 if len(rest) == 1 else F32
    (mine,) = call(add_kernel, [], [keep, received], [(part, wire)], name="pair_sum")
    for step, (tile_bit, dev_bit) in enumerate(rest):
        other = swap(mine, tile_bit, dev_bit)
        kind = BF16 if step == len(rest) - 1 else wire
        (mine,) = call(add_kernel, [], [mine, other], [(part, kind)], name="far_sum")
    other = swap(mine, 0, 2)
    (mine,) = call(join_kernel, [], [mine, other], [(small, BF16)], name="pair_join")
    others = [swap(mine, 2, 0), swap(mine, 0, 1), swap(mine, 2, 1)]
    (mine,) = call(
        quad_join_kernel, [], [mine, *others], [((count, rows, channels), BF16)],
        name="quad_join",
    )
    other = swap(mine, 1, 0)
    whole = ((OFFSETS * channels, channels), F32)
    (grad,) = call(
        functools.partial(finish_kernel, scale), [], [mine, other], [], [whole, 3], [whole],
        name="finish",
    )
    return grad


def per_device(features, morton_pos, neighbours, rim, cotangent, weight_one, weight_two):
    blocks, voxels, channels = features.shape
    rims = rim.shape[0]
    peers = lax.axis_size("dev")
    tiles = lax.axis_size("tile")
    capacity = 2 * ((blocks + peers - 1) // peers)
    block = ((blocks, voxels, channels), BF16)
    rows = blocks * voxels
    depth = OFFSETS * channels
    near = ((blocks, OFFSETS), jnp.int32)
    table = ((blocks + 4 * rims + 1, voxels, channels), F32)
    cells = ((CELLS * blocks, channels), F32)
    columns = ((rows, depth), BF16)
    weight = ((depth, channels), BF16)
    flat = ((rows, channels), F32)
    rim_shape = (rims, voxels, channels)
    macs = rows * depth * channels

    outgoing, cot_rim, rim_tiles = call(
        pack_kernel, [morton_pos, rim, features, cotangent], [],
        [((peers, capacity * voxels + LABEL_ROWS, channels), BF16), (rim_shape, BF16),
         ((rims, 8, channels), F32)],
        [((blocks,), jnp.int32), ((rims,), jnp.int32), block, block, 4], name="pack",
    )
    arrived = lax.all_to_all(outgoing, "dev", split_axis=0, concat_axis=0, tiled=True)
    cot_sides = halo(cot_rim)
    grad_columns, hidden_grad = call(
        first_kernel, [neighbours, cotangent, weight_two], cot_sides, [columns, flat],
        [near, block, weight, table, cells, 3], flops=2 * macs, name="hidden_grad",
    )
    morton, morton_rim, labels = call(
        unpack_kernel, [], [arrived, rim_tiles],
        [block, (rim_shape, BF16), ((peers * capacity, 8, channels), F32)], flops=2 * WAIT, name="unpack",
    )
    sides = halo(morton_rim)
    padded = (OFFSETS + 1, channels // 2, channels)
    hidden, pre_grad, rim_rows, keep_two, send_two, keep_one, send_one = call(
        middle_kernel, [neighbours, rim, weight_one], [morton, *sides, grad_columns, hidden_grad],
        [block, block, ((2,) + rim_shape, BF16)] + [(padded, F32)] * 4,
        [near, ((rims,), jnp.int32), weight, table, cells, columns, flat, flat, 3],
        flops=6 * macs, name="middle",
    )
    scale = 1.0 / math.sqrt(blocks * voxels * tiles * peers)
    grad_two = reduce_all(keep_two, send_two, scale)
    grad_one = reduce_all(keep_one, send_one, scale)
    sides = halo(rim_rows)
    (returning,) = call(
        back_kernel, [neighbours, cotangent, weight_one], [pre_grad, *sides, labels],
        [((peers, capacity * voxels, channels), BF16)],
        [near, block, weight, table, cells, columns, flat, 3], flops=2 * macs, name="back",
    )
    coming_back = lax.all_to_all(returning, "dev", split_axis=0, concat_axis=0, tiled=True)
    output, flat_tiles = call(
        functools.partial(output_kernel, capacity), [neighbours, morton_pos, weight_two],
        [hidden, morton, *sides], [block, ((blocks, 8, channels), F32)],
        [near, ((blocks,), jnp.int32), weight, table, cells, columns, flat, 3], flops=2 * macs, name="output",
    )
    (input_grad,) = call(
        restore_kernel, [], [coming_back.reshape(peers * capacity, voxels, channels), flat_tiles],
        [block], name="restore",
    )
    return (output, input_grad, grad_one, grad_two)


def solution(mesh):
    placed = (
        P(("tile", "dev"), None, None),
        P(("tile", "dev")),
        P(("tile", "dev"), None),
        P(("tile", "dev")),
        P(("tile", "dev"), None, None),
        P(),
        P(),
    )
    return jax.shard_map(
        per_device,
        mesh=mesh,
        in_specs=placed,
        out_specs=(P(("tile", "dev"), None, None), P(("tile", "dev"), None, None), P(), P()),
        check_vma=False,
    )
```

```python
import functools
import math

import jax
import jax.numpy as jnp
from jax import lax
from jax.experimental import pallas as pl
from jax.experimental.pallas import tpu as pltpu
from jax.sharding import PartitionSpec as P

EDGE = 4
OFFSETS = 27
LABEL_ROWS = 16
WAIT = 1_500_000_000
BF16 = jnp.bfloat16
F32 = jnp.float32


def cube_plan():
    cell = {}
    for i in range(EDGE):
        for j in range(EDGE):
            for k in range(EDGE):
                cell[(i + 1, j + 1, k + 1)] = (i * EDGE + j) * EDGE + k
    copies = []
    free = EDGE**3
    for offset in range(OFFSETS):
        steps = (offset // 9 - 1, offset // 3 % 3 - 1, offset % 3 - 1)
        if steps == (0, 0, 0):
            continue
        ranges = [
            {-1: [(0, EDGE - 1)], 0: [(u + 1, u) for u in range(EDGE)], 1: [(EDGE + 1, 0)]}[step]
            for step in steps
        ]
        sources = []
        for x, i in ranges[0]:
            for y, j in ranges[1]:
                for z, k in ranges[2]:
                    cell[(x, y, z)] = free + len(sources)
                    sources.append((i * EDGE + j) * EDGE + k)
        at = 0
        while at < len(sources):
            count, stride = 1, 1
            if at + 1 < len(sources):
                stride = sources[at + 1] - sources[at]
                while (
                    at + count < len(sources)
                    and sources[at + count] - sources[at + count - 1] == stride
                ):
                    count += 1
            if count == 1:
                stride = 1
            copies.append((offset, sources[at], count, stride, free + at))
            at += count
        free += len(sources)
    return cell, copies, free


CELL, COPIES, CELLS = cube_plan()


def cell_runs(offset, flip):
    steps = (offset // 9, offset // 3 % 3, offset % 3)
    if flip:
        steps = tuple(2 - step for step in steps)
    runs = []
    for i in range(EDGE):
        for j in range(EDGE):
            for k in range(EDGE):
                at = CELL[(i + steps[0], j + steps[1], k + steps[2])]
                if runs and runs[-1][0] + runs[-1][1] == at:
                    runs[-1][1] += 1
                else:
                    runs.append([at, 1])
    return runs


def parity(axis, bit=0):
    return (lax.axis_index(axis) >> bit) & 1


def fill_table(table, own, sides, at=None):
    blocks = own.shape[0]
    rims = sides[0].shape[0] if at is None else sides[0].shape[1]
    tile_odd = parity("tile")
    dev_odd = parity("dev")
    firsts = (
        blocks + rims * (1 - tile_odd),
        blocks + rims * tile_odd,
        blocks + rims * (3 - dev_odd),
        blocks + rims * (2 + dev_odd),
    )
    table[0:blocks] = own[...].astype(F32)
    for first, side in zip(firsts, sides):
        table[pl.ds(first, rims)] = (side[...] if at is None else side[at]).astype(F32)
    table[blocks + 4 * rims] = jnp.zeros(table.shape[1:], F32)


def fill_cells(cells, table, near, blocks):
    voxels = table.shape[1]
    for a in range(blocks):
        cells[pl.ds(a, voxels, stride=blocks), :] = table[a]
        for offset, first, count, stride, at in COPIES:
            e = near[a, offset]
            source = pl.ds(first, count) if stride == 1 else pl.ds(first, count, stride=stride)
            if count == 1:
                cells[pl.ds(at * blocks + a, 1), :] = table[e, source, :]
            else:
                cells[pl.ds(at * blocks + a, count, stride=blocks), :] = table[e, source, :]


def fill_columns(columns, cells, blocks, flip):
    channels = cells.shape[1]
    for offset in range(OFFSETS):
        parts = [
            cells[pl.ds(at * blocks, count * blocks), :] for at, count in cell_runs(offset, flip)
        ]
        columns[:, offset * channels : (offset + 1) * channels] = jnp.concatenate(
            parts, axis=0
        ).astype(BF16)


def flipped_dot(columns, weight):
    channels = weight.shape[1]
    total = jnp.zeros((columns.shape[0], channels), F32)
    for offset in range(OFFSETS):
        part = slice(offset * channels, (offset + 1) * channels)
        total = total + lax.dot_general(
            columns[:, part], weight[part, :], (((1,), (1,)), ((), ())), preferred_element_type=F32
        )
    return total


def fetch(sems, *pairs):
    copies = [
        pltpu.make_async_copy(source, target, sems.at[n])
        for n, (source, target) in enumerate(pairs)
    ]
    for copy in copies:
        copy.start()
    return copies


def places_of(morton_pos, blocks):
    devs = [lax.div(morton_pos[r], blocks) for r in range(blocks)]
    places = []
    for r in range(blocks):
        place = jnp.int32(0)
        for earlier in range(r):
            place = place + (devs[earlier] == devs[r]).astype(jnp.int32)
        places.append(place)
    return devs, places


def pack_kernel(
    morton_hbm, rim_hbm, features_hbm, cotangent_hbm,
    outgoing, rim_rows, morton_pos, rim, features, cotangent, sems,
):
    blocks, voxels, channels = features.shape
    peers, rows, _ = outgoing.shape
    capacity = (rows - LABEL_ROWS) // voxels
    copies = fetch(
        sems, (morton_hbm, morton_pos), (features_hbm, features), (rim_hbm, rim),
        (cotangent_hbm, cotangent),
    )
    outgoing[...] = jnp.zeros(outgoing.shape, BF16)
    for p in range(peers):
        outgoing[p, capacity * voxels :, :] = jnp.full((LABEL_ROWS, channels), blocks, BF16)
    row = lax.broadcasted_iota(jnp.int32, (LABEL_ROWS, channels), 0)
    copies[0].wait()
    devs, places = places_of(morton_pos, blocks)
    copies[1].wait()
    for r in range(blocks):
        slot = morton_pos[r] - devs[r] * blocks
        place = places[r]
        outgoing[devs[r], pl.ds(pl.multiple_of(place * voxels, voxels), voxels), :] = features[r]
        held = outgoing[devs[r], capacity * voxels :, :].astype(F32)
        outgoing[devs[r], capacity * voxels :, :] = jnp.where(
            row == place, slot.astype(F32), held
        ).astype(BF16)
    copies[2].wait()
    copies[3].wait()
    for h in range(rim_rows.shape[0]):
        rim_rows[h] = cotangent[rim[h]]


def tiles_of(rows):
    return rows.astype(F32).reshape(-1, 8, rows.shape[-1])


def unpack_kernel(rim_hbm, arrived, morton, rim_rows, labels, rim, sems):
    blocks, voxels, channels = morton.shape
    copies = fetch(sems, (rim_hbm, rim))
    peers, rows, _ = arrived.shape
    capacity = (rows - LABEL_ROWS) // voxels
    held = [jnp.zeros((voxels // 8, 8, channels), F32) for _ in range(blocks)]
    for p in range(peers):
        for c in range(capacity):
            label = jnp.broadcast_to(
                arrived[p, capacity * voxels :, :].astype(F32)[c : c + 1], (8, channels)
            )
            labels[p * capacity + c] = label
            block = tiles_of(arrived[p, c * voxels : (c + 1) * voxels, :])
            for r in range(blocks):
                held[r] = jnp.where((label == r)[None], block, held[r])
    for r in range(blocks):
        morton[r] = held[r].reshape(voxels, channels).astype(BF16)
    copies[0].wait()
    for h in range(rim_rows.shape[0]):
        rim_rows[h] = morton[rim[h]]


def first_kernel(
    near_hbm, cotangent, weight, side_a, side_b, side_c, side_d,
    columns, hidden_grad, near, table, cells, sems,
):
    blocks = cotangent.shape[0]
    copies = fetch(sems, (near_hbm, near))
    fill_table(table, cotangent, (side_a, side_b, side_c, side_d))
    copies[0].wait()
    fill_cells(cells, table, near, blocks)
    fill_columns(columns, cells, blocks, True)
    hidden_grad[...] = flipped_dot(columns, weight)


def middle_kernel(
    near_hbm, rim_hbm, weight, morton, side_a, side_b, side_c, side_d,
    hidden_grad, hidden, pre_grad, rim_rows, columns, turned_hidden, turned_grad,
    near, rim, table, cells, hidden_va, pre_grad_va, sems,
):
    blocks, voxels, channels = morton.shape
    copies = fetch(sems, (near_hbm, near), (rim_hbm, rim))
    fill_table(table, morton, (side_a, side_b, side_c, side_d))
    copies[0].wait()
    fill_cells(cells, table, near, blocks)
    fill_columns(columns, cells, blocks, False)
    copies[1].wait()
    pre_one = jnp.dot(columns[...], weight[...], preferred_element_type=F32)
    gate = jax.nn.sigmoid(pre_one)
    hidden_flat = (pre_one * gate).astype(BF16)
    pre_grad_flat = (hidden_grad[...] * gate * (1.0 + pre_one * (1.0 - gate))).astype(BF16)
    hidden_va[...] = hidden_flat.astype(F32)
    pre_grad_va[...] = pre_grad_flat.astype(F32)
    for a in range(blocks):
        hidden[a] = hidden_va[pl.ds(a, voxels, stride=blocks), :].astype(BF16)
        pre_grad[a] = pre_grad_va[pl.ds(a, voxels, stride=blocks), :].astype(BF16)
    for h in range(rim_rows.shape[1]):
        rim_rows[0, h] = hidden[rim[h]]
        rim_rows[1, h] = pre_grad[rim[h]]
    turned_grad[...] = pre_grad_flat.T
    turned_hidden[...] = hidden_flat.T


def weight_sums_kernel(start, turned_hidden, turned_grad, grad_columns, columns, keep, send):
    channels = turned_grad.shape[0]
    low = jnp.full((channels, channels), parity("tile"), jnp.int32) == 0
    stop = min(start + keep.shape[0], OFFSETS)
    for offset in range(start, stop, 2):
        count = min(2, stop - offset)
        part = slice(offset * channels, (offset + count) * channels)
        two = jnp.dot(turned_hidden[...], grad_columns[:, part], preferred_element_type=F32)
        one = jnp.dot(turned_grad[...], columns[:, part], preferred_element_type=F32)
        for u in range(count):
            part = slice(u * channels, (u + 1) * channels)
            at = offset + u - start
            keep[at] = jnp.where(low, two[:, part], one[:, part].T)
            send[at] = jnp.where(low, one[:, part].T, two[:, part])
    for at in range(stop - start, keep.shape[0]):
        keep[at] = jnp.zeros(keep.shape[1:], F32)
        send[at] = jnp.zeros(send.shape[1:], F32)


def back_kernel(
    near_hbm, cotangent, weight, pre_grad, side_a, side_b, side_c, side_d, labels,
    returning, near, table, cells, columns, result, sems,
):
    blocks, voxels, channels = cotangent.shape
    peers, rows, _ = returning.shape
    capacity = rows // voxels
    copies = fetch(sems, (near_hbm, near))
    fill_table(table, pre_grad, (side_a, side_b, side_c, side_d), 1)
    copies[0].wait()
    fill_cells(cells, table, near, blocks)
    fill_columns(columns, cells, blocks, True)
    result[...] = flipped_dot(columns, weight)
    natural = [
        tiles_of(result[pl.ds(a, voxels, stride=blocks), :] + cotangent[a].astype(F32))
        for a in range(blocks)
    ]
    for p in range(peers):
        for c in range(capacity):
            label = labels[p * capacity + c]
            block = natural[0]
            for r in range(1, blocks):
                block = jnp.where((label == r)[None], natural[r], block)
            returning[p, c * voxels : (c + 1) * voxels, :] = block.reshape(
                voxels, channels
            ).astype(BF16)


def output_kernel(
    capacity, near_hbm, morton_hbm, weight, hidden, morton, side_a, side_b, side_c, side_d,
    output, flat_tiles, near, morton_pos, table, cells, columns, result, sems,
):
    blocks, voxels, channels = morton.shape
    copies = fetch(sems, (near_hbm, near), (morton_hbm, morton_pos))
    fill_table(table, hidden, (side_a, side_b, side_c, side_d), 0)
    copies[0].wait()
    fill_cells(cells, table, near, blocks)
    fill_columns(columns, cells, blocks, False)
    result[...] = jnp.dot(columns[...], weight[...], preferred_element_type=F32)
    for a in range(blocks):
        output[a] = (
            morton[a].astype(F32) + result[pl.ds(a, voxels, stride=blocks), :]
        ).astype(BF16)
    copies[1].wait()
    devs, places = places_of(morton_pos, blocks)
    for r in range(blocks):
        flat_tiles[r] = jnp.full(
            flat_tiles.shape[1:], (devs[r] * capacity + places[r]).astype(F32), F32
        )


def restore_kernel(coming_back, flat_tiles, input_grad):
    blocks, voxels, channels = input_grad.shape
    slots = coming_back.shape[0]
    held = [jnp.zeros((voxels // 8, 8, channels), F32) for _ in range(blocks)]
    for s in range(slots):
        block = tiles_of(coming_back[s])
        for r in range(blocks):
            held[r] = jnp.where((flat_tiles[r] == s)[None], block, held[r])
    for r in range(blocks):
        input_grad[r] = held[r].reshape(voxels, channels).astype(BF16)


def order_bits(group):
    x, y = parity("tile", 1), parity("dev")
    turned = (parity("tile") + group) & 1
    return jnp.where(turned == 0, x, y), jnp.where(turned == 0, y, x)


def step_bit(step, group):
    return order_bits(group)[step] if step < 2 else parity("dev", 1)


def half(rows, index):
    return pl.ds(pl.multiple_of(index * rows, rows), rows)


def split_kernel(step, group, mine, other, keep, send):
    rows = keep.shape[1]
    bit = step_bit(step, group)
    for ref, index in ((keep, bit), (send, 1 - bit)):
        at = half(rows, index)
        ref[...] = (mine[:, at, :] + other[:, at, :].astype(F32)).astype(ref.dtype)


def add_kernel(left, right, total):
    total[...] = (left[...].astype(F32) + right[...].astype(F32)).astype(total.dtype)


def join_kernel(step, group, mine, other, joined):
    rows = mine.shape[1]
    bit = step_bit(step, group)
    joined[:, half(rows, bit), :] = mine[...]
    joined[:, half(rows, 1 - bit), :] = other[...]


def write_gradient(scale, parts, grad_hbm, grad, sems):
    channels = grad.shape[1]
    copies = []
    for n, ref in enumerate(parts):
        start = n * ref.shape[0]
        count = min(ref.shape[0], OFFSETS - start)
        for u in range(count):
            grad[pl.ds((start + u) * channels, channels), :] = ref[u].astype(F32) * scale
        part = pl.ds(start * channels, count * channels)
        copies.append((grad.at[part], grad_hbm.at[part], sems.at[n]))
    for copy in copies:
        pltpu.make_async_copy(*copy).start()
    for copy in copies:
        pltpu.make_async_copy(*copy).wait()


def finish_kernel(scale, owner, *refs):
    *parts, one_hbm, two_hbm, grad, sems = refs

    @pl.when(parity("tile") == owner)
    def _():
        write_gradient(scale, parts[-2:], two_hbm, grad, sems)

    @pl.when(parity("tile") != owner)
    def _():
        write_gradient(scale, parts[-2:], one_hbm, grad, sems)


HBM = pl.BlockSpec(memory_space=pltpu.HBM)
ANY = pl.BlockSpec(memory_space=pl.ANY)
VMEM = pl.BlockSpec(memory_space=pltpu.VMEM)


def call(kernel, far, arrays, outs, scratch=(), far_outs=(), flops=0, name=None, after=(), aliases={}):
    shapes = [jax.ShapeDtypeStruct(shape, dtype) for shape, dtype in [*outs, *far_outs]]
    moved = sum(x.size * x.dtype.itemsize for x in [*far, *arrays])
    moved += sum(math.prod(s.shape) * s.dtype.itemsize for s in shapes)
    held = []
    for item in scratch:
        if isinstance(item, int):
            held.append(pltpu.SemaphoreType.DMA((item,)))
        else:
            held.append((pltpu.SMEM if item[1] == jnp.int32 else pltpu.VMEM)(*item))
    body = kernel
    if after:

        def body(*refs):
            kernel(*refs[len(after) :])

    return pl.pallas_call(
        body,
        out_shape=shapes,
        in_specs=[ANY] * len(after) + [HBM] * len(far) + [VMEM] * len(arrays),
        out_specs=[VMEM] * len(outs) + [HBM] * len(far_outs),
        scratch_shapes=held,
        input_output_aliases=aliases,
        compiler_params=pltpu.CompilerParams(vmem_limit_bytes=(63 if name == "pack" else 24) * 2**20),
        cost_estimate=pl.CostEstimate(flops=flops, bytes_accessed=moved, transcendentals=0),
        name=name,
    )(*after, *far, *arrays)


def halo(rows):
    sides = []
    for axis in ("tile", "dev"):
        count = lax.axis_size(axis)
        even = [(i, i ^ 1) for i in range(count)]
        odd = []
        for i in range(1, count - 1, 2):
            odd += [(i, i + 1), (i + 1, i)]
        sides += [lax.ppermute(rows, axis, even), lax.ppermute(rows, axis, odd)]
    return sides


def swap(rows, partner):
    tiles, devs = lax.axis_size("tile"), lax.axis_size("dev")
    pairs = []
    for t in range(tiles):
        for d in range(devs):
            other = partner(t, d)
            pairs.append((t * devs + d, other[0] * devs + other[1]))
    return lax.ppermute(rows, ("tile", "dev"), pairs)


def other_core(t, d):
    return t ^ 1, d


def partner_at(step, group):
    def partner(t, d):
        if step == 2:
            return t, d ^ 2
        along_x = ((t + group) & 1) == step
        return (t ^ 2, d) if along_x else (t, d ^ 1)

    return partner


def split_stage(step, group, mine, other, wire, after=()):
    count, rows, channels = mine.shape
    part = (count, rows // 2, channels)
    return call(
        functools.partial(split_kernel, step, group), [], [mine, other],
        [(part, F32), (part, wire)], name="split", after=after,
    )


def pair_stage(keep, send, wire, after=()):
    (mine,) = call(
        add_kernel, [], [keep, swap(send, partner_at(2, 0))], [(keep.shape, wire)],
        name="pair_sum", after=after,
    )
    return mine


def far_steps():
    rest = [(0, 1 << bit) for bit in range(2, lax.axis_size("dev").bit_length() - 1)]
    rest += [(1 << bit, 0) for bit in range(2, lax.axis_size("tile").bit_length() - 1)]
    return rest


def far_stage(mine, after=()):
    rest = far_steps()
    for step, bits in enumerate(rest):
        kind = BF16 if step == len(rest) - 1 else mine.dtype
        other = swap(mine, lambda t, d, bits=bits: (t ^ bits[0], d ^ bits[1]))
        (mine,) = call(
            add_kernel, [], [mine, other], [(mine.shape, kind)], name="far_sum", after=after
        )
        after = ()
    return mine


def join_stage(step, group, mine, after=()):
    count, rows, channels = mine.shape
    (mine,) = call(
        functools.partial(join_kernel, step, group), [], [mine, swap(mine, partner_at(step, group))],
        [((count, 2 * rows, channels), BF16)], name="join", after=after,
    )
    return mine


def finish(scale, owner, parts, held=(), after=()):
    channels = parts[0].shape[2]
    whole = ((OFFSETS * channels, channels), F32)
    first = len(after)
    return call(
        functools.partial(finish_kernel, scale, owner), held, parts, [], [whole, 2],
        [whole, whole], name="finish", after=after,
        aliases={first: 0, first + 1: 1} if held else {},
    )


def per_device(features, morton_pos, neighbours, rim, cotangent, weight_one, weight_two):
    blocks, voxels, channels = features.shape
    rims = rim.shape[0]
    peers = lax.axis_size("dev")
    tiles = lax.axis_size("tile")
    capacity = 2 * ((blocks + peers - 1) // peers)
    block = ((blocks, voxels, channels), BF16)
    rows = blocks * voxels
    depth = OFFSETS * channels
    near = ((blocks, OFFSETS), jnp.int32)
    table = ((blocks + 4 * rims + 1, voxels, channels), F32)
    cells = ((CELLS * blocks, channels), F32)
    columns = ((rows, depth), BF16)
    flat = ((rows, channels), F32)
    rim_shape = (rims, voxels, channels)
    macs = rows * depth * channels

    outgoing, cot_rim = call(
        pack_kernel, [morton_pos, rim, features, cotangent], [],
        [((peers, capacity * voxels + LABEL_ROWS, channels), BF16), (rim_shape, BF16)],
        [((blocks,), jnp.int32), ((rims,), jnp.int32), block, block, 4], flops=WAIT, name="pack",
    )
    arrived = lax.all_to_all(outgoing, "dev", split_axis=0, concat_axis=0, tiled=True)
    cot_sides = halo(cot_rim)
    grad_columns, hidden_grad = call(
        first_kernel, [neighbours], [cotangent, weight_two, *cot_sides], [columns, flat],
        [near, table, cells, 1], flops=2 * macs, name="hidden_grad",
    )
    morton, morton_rim, labels = call(
        unpack_kernel, [rim], [arrived],
        [block, (rim_shape, BF16), ((peers * capacity, 8, channels), F32)],
        [((rims,), jnp.int32), 1], flops=4 * WAIT, name="unpack",
    )
    sides = halo(morton_rim)
    hidden, pre_grad, rim_rows, morton_columns, turned_hidden, turned_grad = call(
        middle_kernel, [neighbours, rim], [weight_one, morton, *sides, hidden_grad],
        [block, block, ((2,) + rim_shape, BF16), columns, ((channels, rows), BF16),
         ((channels, rows), BF16)],
        [near, ((rims,), jnp.int32), table, cells, flat, flat, 2],
        flops=2 * macs, name="middle",
    )
    count = (OFFSETS + 1) // 2
    groups = range(2)
    wire = BF16 if len(far_steps()) == 1 else F32
    parts = [
        call(
            functools.partial(weight_sums_kernel, group * count), [],
            [turned_hidden, turned_grad, grad_columns, morton_columns],
            [((count, channels, channels), F32)] * 2, flops=2 * macs, name="weight_sums",
        )
        for group in groups
    ]
    scale = 1.0 / math.sqrt(blocks * voxels * tiles * peers)
    sides = halo(rim_rows)
    parts = [
        split_stage(0, g, parts[g][0], swap(parts[g][1], other_core), BF16)
        for g in groups
    ]
    parts = [
        split_stage(1, g, parts[g][0], swap(parts[g][1], partner_at(0, g)), BF16)
        for g in groups
    ]
    output, flat_tiles = call(
        functools.partial(output_kernel, capacity), [neighbours, morton_pos],
        [weight_two, hidden, morton, *sides], [block, ((blocks, 8, channels), F32)],
        [near, ((blocks,), jnp.int32), table, cells, columns, flat, 2], flops=2 * macs,
        name="output",
    )
    (returning,) = call(
        back_kernel, [neighbours], [cotangent, weight_one, pre_grad, *sides, labels],
        [((peers, capacity * voxels, channels), BF16)],
        [near, table, cells, columns, flat, 1], flops=2 * macs, name="back",
    )
    parts = [
        split_stage(2, g, parts[g][0], swap(parts[g][1], partner_at(1, g)), F32, after=sides if g == 1 else ())
        for g in groups
    ]
    parts = [pair_stage(*parts[g], wire, after=[returning] if g == 1 else ()) for g in groups]
    parts = [far_stage(parts[g]) for g in groups]
    coming_back = lax.all_to_all(returning, "dev", split_axis=0, concat_axis=0, tiled=True)
    parts = [join_stage(2, g, parts[g], after=[flat_tiles] if g == 1 else ()) for g in groups]
    parts = [join_stage(1, g, parts[g]) for g in groups]
    (input_grad,) = call(
        restore_kernel, [], [coming_back.reshape(peers * capacity, voxels, channels), flat_tiles],
        [block], name="restore",
    )
    parts = [join_stage(0, g, parts[g], after=[coming_back] if g == 1 else ()) for g in groups]
    others = [swap(parts[g], other_core) for g in groups]
    grads = finish(scale, 0, parts)
    grad_one, grad_two = finish(scale, 1, others, grads)
    return (output, input_grad, grad_one, grad_two)


def solution(mesh):
    placed = (
        P(("tile", "dev"), None, None),
        P(("tile", "dev")),
        P(("tile", "dev"), None),
        P(("tile", "dev")),
        P(("tile", "dev"), None, None),
        P(),
        P(),
    )
    return jax.shard_map(
        per_device,
        mesh=mesh,
        in_specs=placed,
        out_specs=(P(("tile", "dev"), None, None), P(("tile", "dev"), None, None), P(), P()),
        check_vma=False,
    )
```

```python
import functools
import math

import jax
import jax.numpy as jnp
from jax import lax
from jax.experimental import pallas as pl
from jax.experimental.pallas import tpu as pltpu
from jax.sharding import PartitionSpec as P

EDGE = 4
OFFSETS = 27
LABEL_ROWS = 16
WAIT = 1_500_000_000
CHUNK = 6
BF16 = jnp.bfloat16
F32 = jnp.float32


def cube_plan():
    cell = {}
    for i in range(EDGE):
        for j in range(EDGE):
            for k in range(EDGE):
                cell[(i + 1, j + 1, k + 1)] = (i * EDGE + j) * EDGE + k
    copies = []
    free = EDGE**3
    for offset in range(OFFSETS):
        steps = (offset // 9 - 1, offset // 3 % 3 - 1, offset % 3 - 1)
        if steps == (0, 0, 0):
            continue
        ranges = [
            {-1: [(0, EDGE - 1)], 0: [(u + 1, u) for u in range(EDGE)], 1: [(EDGE + 1, 0)]}[step]
            for step in steps
        ]
        sources = []
        for x, i in ranges[0]:
            for y, j in ranges[1]:
                for z, k in ranges[2]:
                    cell[(x, y, z)] = free + len(sources)
                    sources.append((i * EDGE + j) * EDGE + k)
        at = 0
        while at < len(sources):
            count, stride = 1, 1
            if at + 1 < len(sources):
                stride = sources[at + 1] - sources[at]
                while (
                    at + count < len(sources)
                    and sources[at + count] - sources[at + count - 1] == stride
                ):
                    count += 1
            if count == 1:
                stride = 1
            copies.append((offset, sources[at], count, stride, free + at))
            at += count
        free += len(sources)
    return cell, copies, free


CELL, COPIES, CELLS = cube_plan()


def cell_runs(offset, flip):
    steps = (offset // 9, offset // 3 % 3, offset % 3)
    if flip:
        steps = tuple(2 - step for step in steps)
    runs = []
    for i in range(EDGE):
        for j in range(EDGE):
            for k in range(EDGE):
                at = CELL[(i + steps[0], j + steps[1], k + steps[2])]
                if runs and runs[-1][0] + runs[-1][1] == at:
                    runs[-1][1] += 1
                else:
                    runs.append([at, 1])
    return runs


def parity(axis, bit=0):
    return (lax.axis_index(axis) >> bit) & 1


def fill_table(table, own, sides, at=None):
    blocks = own.shape[0]
    rims = sides[0].shape[0] if at is None else sides[0].shape[1]
    tile_odd = parity("tile")
    dev_odd = parity("dev")
    firsts = (
        blocks + rims * (1 - tile_odd),
        blocks + rims * tile_odd,
        blocks + rims * (3 - dev_odd),
        blocks + rims * (2 + dev_odd),
    )
    table[0:blocks] = own[...].astype(F32)
    for first, side in zip(firsts, sides):
        table[pl.ds(first, rims)] = (side[...] if at is None else side[at]).astype(F32)
    table[blocks + 4 * rims] = jnp.zeros(table.shape[1:], F32)


def fill_cells(cells, table, near, blocks):
    voxels = table.shape[1]
    for a in range(blocks):
        cells[pl.ds(a, voxels, stride=blocks), :] = table[a]
        for offset, first, count, stride, at in COPIES:
            e = near[a, offset]
            source = pl.ds(first, count) if stride == 1 else pl.ds(first, count, stride=stride)
            if count == 1:
                cells[pl.ds(at * blocks + a, 1), :] = table[e, source, :]
            else:
                cells[pl.ds(at * blocks + a, count, stride=blocks), :] = table[e, source, :]


def fill_columns(columns, cells, blocks, flip):
    channels = cells.shape[1]
    for offset in range(OFFSETS):
        parts = [
            cells[pl.ds(at * blocks, count * blocks), :] for at, count in cell_runs(offset, flip)
        ]
        columns[:, offset * channels : (offset + 1) * channels] = jnp.concatenate(
            parts, axis=0
        ).astype(BF16)


def flipped_dot(columns, weight):
    channels = weight.shape[1]
    total = jnp.zeros((columns.shape[0], channels), F32)
    for offset in range(OFFSETS):
        part = slice(offset * channels, (offset + 1) * channels)
        total = total + lax.dot_general(
            columns[:, part], weight[part, :], (((1,), (1,)), ((), ())), preferred_element_type=F32
        )
    return total


def fetch(sems, *pairs):
    copies = [
        pltpu.make_async_copy(source, target, sems.at[n])
        for n, (source, target) in enumerate(pairs)
    ]
    for copy in copies:
        copy.start()
    return copies


def places_of(morton_pos, blocks):
    devs = [lax.div(morton_pos[r], blocks) for r in range(blocks)]
    places = []
    for r in range(blocks):
        place = jnp.int32(0)
        for earlier in range(r):
            place = place + (devs[earlier] == devs[r]).astype(jnp.int32)
        places.append(place)
    return devs, places


def pack_kernel(
    morton_hbm, rim_hbm, features_hbm, cotangent_hbm,
    outgoing, rim_rows, morton_pos, rim, features, cotangent, sems,
):
    blocks, voxels, channels = features.shape
    peers, rows, _ = outgoing.shape
    capacity = (rows - LABEL_ROWS) // voxels
    copies = fetch(
        sems, (morton_hbm, morton_pos), (features_hbm, features), (rim_hbm, rim),
        (cotangent_hbm, cotangent),
    )
    outgoing[...] = jnp.zeros(outgoing.shape, BF16)
    for p in range(peers):
        outgoing[p, capacity * voxels :, :] = jnp.full((LABEL_ROWS, channels), blocks, BF16)
    row = lax.broadcasted_iota(jnp.int32, (LABEL_ROWS, channels), 0)
    copies[0].wait()
    devs, places = places_of(morton_pos, blocks)
    copies[1].wait()
    for r in range(blocks):
        slot = morton_pos[r] - devs[r] * blocks
        place = places[r]
        outgoing[devs[r], pl.ds(pl.multiple_of(place * voxels, voxels), voxels), :] = features[r]
        held = outgoing[devs[r], capacity * voxels :, :].astype(F32)
        outgoing[devs[r], capacity * voxels :, :] = jnp.where(
            row == place, slot.astype(F32), held
        ).astype(BF16)
    copies[2].wait()
    copies[3].wait()
    for h in range(rim_rows.shape[0]):
        rim_rows[h] = cotangent[rim[h]]


def tiles_of(rows):
    return rows.astype(F32).reshape(-1, 8, rows.shape[-1])


def unpack_kernel(rim_hbm, arrived, morton, rim_rows, labels, rim, sems):
    blocks, voxels, channels = morton.shape
    copies = fetch(sems, (rim_hbm, rim))
    peers, rows, _ = arrived.shape
    capacity = (rows - LABEL_ROWS) // voxels
    held = [jnp.zeros((voxels // 8, 8, channels), F32) for _ in range(blocks)]
    for p in range(peers):
        for c in range(capacity):
            label = jnp.broadcast_to(
                arrived[p, capacity * voxels :, :].astype(F32)[c : c + 1], (8, channels)
            )
            labels[p * capacity + c] = label
            block = tiles_of(arrived[p, c * voxels : (c + 1) * voxels, :])
            for r in range(blocks):
                held[r] = jnp.where((label == r)[None], block, held[r])
    for r in range(blocks):
        morton[r] = held[r].reshape(voxels, channels).astype(BF16)
    copies[0].wait()
    for h in range(rim_rows.shape[0]):
        rim_rows[h] = morton[rim[h]]


def first_kernel(
    near_hbm, cotangent, weight, side_a, side_b, side_c, side_d,
    columns, hidden_grad, near, table, cells, sems,
):
    blocks = cotangent.shape[0]
    copies = fetch(sems, (near_hbm, near))
    fill_table(table, cotangent, (side_a, side_b, side_c, side_d))
    copies[0].wait()
    fill_cells(cells, table, near, blocks)
    fill_columns(columns, cells, blocks, True)
    hidden_grad[...] = flipped_dot(columns, weight)


def middle_kernel(
    near_hbm, rim_hbm, weight, morton, side_a, side_b, side_c, side_d,
    hidden_grad, hidden, pre_grad, rim_rows, columns, turned_hidden, turned_grad,
    near, rim, table, cells, hidden_va, pre_grad_va, sems,
):
    blocks, voxels, channels = morton.shape
    copies = fetch(sems, (near_hbm, near), (rim_hbm, rim))
    fill_table(table, morton, (side_a, side_b, side_c, side_d))
    copies[0].wait()
    fill_cells(cells, table, near, blocks)
    fill_columns(columns, cells, blocks, False)
    copies[1].wait()
    pre_one = jnp.dot(columns[...], weight[...], preferred_element_type=F32)
    gate = jax.nn.sigmoid(pre_one)
    hidden_flat = (pre_one * gate).astype(BF16)
    pre_grad_flat = (hidden_grad[...] * gate * (1.0 + pre_one * (1.0 - gate))).astype(BF16)
    hidden_va[...] = hidden_flat.astype(F32)
    pre_grad_va[...] = pre_grad_flat.astype(F32)
    for a in range(blocks):
        hidden[a] = hidden_va[pl.ds(a, voxels, stride=blocks), :].astype(BF16)
        pre_grad[a] = pre_grad_va[pl.ds(a, voxels, stride=blocks), :].astype(BF16)
    for h in range(rim_rows.shape[1]):
        rim_rows[0, h] = hidden[rim[h]]
        rim_rows[1, h] = pre_grad[rim[h]]
    turned_grad[...] = pre_grad_flat.T
    turned_hidden[...] = hidden_flat.T


def weight_sums_kernel(start, turned_hidden, turned_grad, grad_columns, columns, keep, send):
    channels = turned_grad.shape[0]
    low = jnp.full((channels, channels), parity("tile"), jnp.int32) == 0
    stop = min(start + keep.shape[0], OFFSETS)
    for offset in range(start, stop, 2):
        count = min(2, stop - offset)
        part = slice(offset * channels, (offset + count) * channels)
        two = jnp.dot(turned_hidden[...], grad_columns[:, part], preferred_element_type=F32)
        one = jnp.dot(turned_grad[...], columns[:, part], preferred_element_type=F32)
        for u in range(count):
            part = slice(u * channels, (u + 1) * channels)
            at = offset + u - start
            keep[at] = jnp.where(low, two[:, part], one[:, part].T)
            send[at] = jnp.where(low, one[:, part].T, two[:, part])
    for at in range(stop - start, keep.shape[0]):
        keep[at] = jnp.zeros(keep.shape[1:], F32)
        send[at] = jnp.zeros(send.shape[1:], F32)


def back_kernel(
    near_hbm, cotangent, weight, pre_grad, side_a, side_b, side_c, side_d, labels,
    returning, near, table, cells, columns, result, sems,
):
    blocks, voxels, channels = cotangent.shape
    peers, rows, _ = returning.shape
    capacity = rows // voxels
    copies = fetch(sems, (near_hbm, near))
    fill_table(table, pre_grad, (side_a, side_b, side_c, side_d), 1)
    copies[0].wait()
    fill_cells(cells, table, near, blocks)
    fill_columns(columns, cells, blocks, True)
    result[...] = flipped_dot(columns, weight)
    natural = [
        tiles_of(result[pl.ds(a, voxels, stride=blocks), :] + cotangent[a].astype(F32))
        for a in range(blocks)
    ]
    for p in range(peers):
        for c in range(capacity):
            label = labels[p * capacity + c]
            block = natural[0]
            for r in range(1, blocks):
                block = jnp.where((label == r)[None], natural[r], block)
            returning[p, c * voxels : (c + 1) * voxels, :] = block.reshape(
                voxels, channels
            ).astype(BF16)


def output_kernel(
    capacity, near_hbm, morton_hbm, weight, hidden, morton, side_a, side_b, side_c, side_d,
    output, flat_tiles, near, morton_pos, table, cells, columns, result, sems,
):
    blocks, voxels, channels = morton.shape
    copies = fetch(sems, (near_hbm, near), (morton_hbm, morton_pos))
    fill_table(table, hidden, (side_a, side_b, side_c, side_d), 0)
    copies[0].wait()
    fill_cells(cells, table, near, blocks)
    fill_columns(columns, cells, blocks, False)
    result[...] = jnp.dot(columns[...], weight[...], preferred_element_type=F32)
    for a in range(blocks):
        output[a] = (
            morton[a].astype(F32) + result[pl.ds(a, voxels, stride=blocks), :]
        ).astype(BF16)
    copies[1].wait()
    devs, places = places_of(morton_pos, blocks)
    for r in range(blocks):
        flat_tiles[r] = jnp.full(
            flat_tiles.shape[1:], (devs[r] * capacity + places[r]).astype(F32), F32
        )


def restore_kernel(coming_back, flat_tiles, input_grad):
    blocks, voxels, channels = input_grad.shape
    slots = coming_back.shape[0]
    held = [jnp.zeros((voxels // 8, 8, channels), F32) for _ in range(blocks)]
    for s in range(slots):
        block = tiles_of(coming_back[s])
        for r in range(blocks):
            held[r] = jnp.where((flat_tiles[r] == s)[None], block, held[r])
    for r in range(blocks):
        input_grad[r] = held[r].reshape(voxels, channels).astype(BF16)


def order_bits(group):
    x, y = parity("tile", 1), parity("dev")
    turned = (parity("tile") + group) & 1
    return jnp.where(turned == 0, x, y), jnp.where(turned == 0, y, x)


def step_bit(step, group):
    return order_bits(group)[step] if step < 2 else parity("dev", 1)


def half(rows, index):
    return pl.ds(pl.multiple_of(index * rows, rows), rows)


def split_kernel(step, group, mine, other, keep, send):
    rows = keep.shape[1]
    bit = step_bit(step, group)
    for ref, index in ((keep, bit), (send, 1 - bit)):
        at = half(rows, index)
        ref[...] = (mine[:, at, :] + other[:, at, :].astype(F32)).astype(ref.dtype)


def add_kernel(left, right, total):
    total[...] = (left[...].astype(F32) + right[...].astype(F32)).astype(total.dtype)


def join_kernel(step, group, mine, other, joined):
    rows = mine.shape[1]
    bit = step_bit(step, group)
    joined[:, half(rows, bit), :] = mine[...]
    joined[:, half(rows, 1 - bit), :] = other[...]


def write_gradient(scale, parts, grad_hbm, grad, sems):
    channels = grad.shape[1]
    copies = []
    for first in range(0, OFFSETS, CHUNK):
        last = min(first + CHUNK, OFFSETS)
        for offset in range(first, last):
            ref = parts[offset // parts[0].shape[0]]
            rows = slice(offset * channels, (offset + 1) * channels)
            grad[rows, :] = ref[offset % ref.shape[0]].astype(F32) * scale
        part = pl.ds(first * channels, (last - first) * channels)
        copies.append(
            pltpu.make_async_copy(grad.at[part], grad_hbm.at[part], sems.at[len(copies)])
        )
        copies[-1].start()
    for copy in copies:
        copy.wait()


def finish_kernel(scale, owner, *refs):
    *parts, one_hbm, two_hbm, grad, sems = refs

    @pl.when(parity("tile") == owner)
    def _():
        write_gradient(scale, parts[-2:], two_hbm, grad, sems)

    @pl.when(parity("tile") != owner)
    def _():
        write_gradient(scale, parts[-2:], one_hbm, grad, sems)


HBM = pl.BlockSpec(memory_space=pltpu.HBM)
ANY = pl.BlockSpec(memory_space=pl.ANY)
VMEM = pl.BlockSpec(memory_space=pltpu.VMEM)


def call(kernel, far, arrays, outs, scratch=(), far_outs=(), flops=0, name=None, after=(), aliases={}):
    shapes = [jax.ShapeDtypeStruct(shape, dtype) for shape, dtype in [*outs, *far_outs]]
    moved = sum(x.size * x.dtype.itemsize for x in [*far, *arrays])
    moved += sum(math.prod(s.shape) * s.dtype.itemsize for s in shapes)
    held = []
    for item in scratch:
        if isinstance(item, int):
            held.append(pltpu.SemaphoreType.DMA((item,)))
        else:
            held.append((pltpu.SMEM if item[1] == jnp.int32 else pltpu.VMEM)(*item))
    body = kernel
    if after:

        def body(*refs):
            kernel(*refs[len(after) :])

    return pl.pallas_call(
        body,
        out_shape=shapes,
        in_specs=[ANY] * len(after) + [HBM] * len(far) + [VMEM] * len(arrays),
        out_specs=[VMEM] * len(outs) + [HBM] * len(far_outs),
        scratch_shapes=held,
        input_output_aliases=aliases,
        compiler_params=pltpu.CompilerParams(vmem_limit_bytes=(63 if name == "pack" else 24) * 2**20),
        cost_estimate=pl.CostEstimate(flops=flops, bytes_accessed=moved, transcendentals=0),
        name=name,
    )(*after, *far, *arrays)


def halo(rows):
    sides = []
    for axis in ("tile", "dev"):
        count = lax.axis_size(axis)
        even = [(i, i ^ 1) for i in range(count)]
        odd = []
        for i in range(1, count - 1, 2):
            odd += [(i, i + 1), (i + 1, i)]
        sides += [lax.ppermute(rows, axis, even), lax.ppermute(rows, axis, odd)]
    return sides


def swap(rows, partner):
    tiles, devs = lax.axis_size("tile"), lax.axis_size("dev")
    pairs = []
    for t in range(tiles):
        for d in range(devs):
            other = partner(t, d)
            pairs.append((t * devs + d, other[0] * devs + other[1]))
    return lax.ppermute(rows, ("tile", "dev"), pairs)


def other_core(t, d):
    return t ^ 1, d


def partner_at(step, group):
    def partner(t, d):
        if step == 2:
            return t, d ^ 2
        along_x = ((t + group) & 1) == step
        return (t ^ 2, d) if along_x else (t, d ^ 1)

    return partner


def split_stage(step, group, mine, other, wire, after=()):
    count, rows, channels = mine.shape
    part = (count, rows // 2, channels)
    return call(
        functools.partial(split_kernel, step, group), [], [mine, other],
        [(part, F32), (part, wire)], name="split", after=after,
    )


def pair_stage(keep, send, wire, after=()):
    (mine,) = call(
        add_kernel, [], [keep, swap(send, partner_at(2, 0))], [(keep.shape, wire)],
        name="pair_sum", after=after,
    )
    return mine


def far_steps():
    rest = [(0, 1 << bit) for bit in range(2, lax.axis_size("dev").bit_length() - 1)]
    rest += [(1 << bit, 0) for bit in range(2, lax.axis_size("tile").bit_length() - 1)]
    return rest


def far_stage(mine, after=()):
    rest = far_steps()
    for step, bits in enumerate(rest):
        kind = BF16 if step == len(rest) - 1 else mine.dtype
        other = swap(mine, lambda t, d, bits=bits: (t ^ bits[0], d ^ bits[1]))
        (mine,) = call(
            add_kernel, [], [mine, other], [(mine.shape, kind)], name="far_sum", after=after
        )
        after = ()
    return mine


def join_stage(step, group, mine, after=()):
    count, rows, channels = mine.shape
    (mine,) = call(
        functools.partial(join_kernel, step, group), [], [mine, swap(mine, partner_at(step, group))],
        [((count, 2 * rows, channels), BF16)], name="join", after=after,
    )
    return mine


def finish(scale, owner, parts, held=(), after=()):
    channels = parts[0].shape[2]
    whole = ((OFFSETS * channels, channels), F32)
    first = len(after)
    return call(
        functools.partial(finish_kernel, scale, owner), held, parts, [],
        [whole, -(-OFFSETS // CHUNK)],
        [whole, whole], name="finish", after=after,
        aliases={first: 0, first + 1: 1} if held else {},
    )


def per_device(features, morton_pos, neighbours, rim, cotangent, weight_one, weight_two):
    blocks, voxels, channels = features.shape
    rims = rim.shape[0]
    peers = lax.axis_size("dev")
    tiles = lax.axis_size("tile")
    capacity = 2 * ((blocks + peers - 1) // peers)
    block = ((blocks, voxels, channels), BF16)
    rows = blocks * voxels
    depth = OFFSETS * channels
    near = ((blocks, OFFSETS), jnp.int32)
    table = ((blocks + 4 * rims + 1, voxels, channels), F32)
    cells = ((CELLS * blocks, channels), F32)
    columns = ((rows, depth), BF16)
    flat = ((rows, channels), F32)
    rim_shape = (rims, voxels, channels)
    macs = rows * depth * channels

    outgoing, cot_rim = call(
        pack_kernel, [morton_pos, rim, features, cotangent], [],
        [((peers, capacity * voxels + LABEL_ROWS, channels), BF16), (rim_shape, BF16)],
        [((blocks,), jnp.int32), ((rims,), jnp.int32), block, block, 4], flops=WAIT, name="pack",
    )
    arrived = lax.all_to_all(outgoing, "dev", split_axis=0, concat_axis=0, tiled=True)
    cot_sides = halo(cot_rim)
    grad_columns, hidden_grad = call(
        first_kernel, [neighbours], [cotangent, weight_two, *cot_sides], [columns, flat],
        [near, table, cells, 1], flops=2 * macs, name="hidden_grad",
    )
    morton, morton_rim, labels = call(
        unpack_kernel, [rim], [arrived],
        [block, (rim_shape, BF16), ((peers * capacity, 8, channels), F32)],
        [((rims,), jnp.int32), 1], flops=4 * WAIT, name="unpack",
    )
    sides = halo(morton_rim)
    hidden, pre_grad, rim_rows, morton_columns, turned_hidden, turned_grad = call(
        middle_kernel, [neighbours, rim], [weight_one, morton, *sides, hidden_grad],
        [block, block, ((2,) + rim_shape, BF16), columns, ((channels, rows), BF16),
         ((channels, rows), BF16)],
        [near, ((rims,), jnp.int32), table, cells, flat, flat, 2],
        flops=2 * macs, name="middle",
    )
    count = (OFFSETS + 1) // 2
    groups = range(2)
    wire = BF16 if len(far_steps()) == 1 else F32
    parts = [
        call(
            functools.partial(weight_sums_kernel, group * count), [],
            [turned_hidden, turned_grad, grad_columns, morton_columns],
            [((count, channels, channels), F32)] * 2, flops=2 * macs, name="weight_sums",
        )
        for group in groups
    ]
    scale = 1.0 / math.sqrt(blocks * voxels * tiles * peers)
    sides = halo(rim_rows)
    parts = [
        split_stage(0, g, parts[g][0], swap(parts[g][1], other_core), BF16)
        for g in groups
    ]
    parts = [
        split_stage(1, g, parts[g][0], swap(parts[g][1], partner_at(0, g)), BF16)
        for g in groups
    ]
    output, flat_tiles = call(
        functools.partial(output_kernel, capacity), [neighbours, morton_pos],
        [weight_two, hidden, morton, *sides], [block, ((blocks, 8, channels), F32)],
        [near, ((blocks,), jnp.int32), table, cells, columns, flat, 2], flops=2 * macs,
        name="output",
    )
    (returning,) = call(
        back_kernel, [neighbours], [cotangent, weight_one, pre_grad, *sides, labels],
        [((peers, capacity * voxels, channels), BF16)],
        [near, table, cells, columns, flat, 1], flops=2 * macs, name="back",
    )
    parts = [
        split_stage(2, g, parts[g][0], swap(parts[g][1], partner_at(1, g)), F32, after=sides[:2] if g == 1 else ())
        for g in groups
    ]
    parts = [pair_stage(*parts[g], wire, after=[returning] if g == 1 else ()) for g in groups]
    parts = [far_stage(parts[g]) for g in groups]
    coming_back = lax.all_to_all(returning, "dev", split_axis=0, concat_axis=0, tiled=True)
    parts = [join_stage(2, g, parts[g], after=[flat_tiles] if g == 1 else ()) for g in groups]
    parts = [join_stage(1, g, parts[g]) for g in groups]
    (input_grad,) = call(
        restore_kernel, [], [coming_back.reshape(peers * capacity, voxels, channels), flat_tiles],
        [block], name="restore",
    )
    parts = [join_stage(0, g, parts[g], after=[coming_back] if g == 1 else ()) for g in groups]
    others = [swap(parts[g], other_core) for g in groups]
    grads = finish(scale, 0, parts)
    grad_one, grad_two = finish(scale, 1, others, grads)
    return (output, input_grad, grad_one, grad_two)


def solution(mesh):
    placed = (
        P(("tile", "dev"), None, None),
        P(("tile", "dev")),
        P(("tile", "dev"), None),
        P(("tile", "dev")),
        P(("tile", "dev"), None, None),
        P(),
        P(),
    )
    return jax.shard_map(
        per_device,
        mesh=mesh,
        in_specs=placed,
        out_specs=(P(("tile", "dev"), None, None), P(("tile", "dev"), None, None), P(), P()),
        check_vma=False,
    )
```

```python
import functools
import math

import jax
import jax.numpy as jnp
from jax import lax
from jax.experimental import pallas as pl
from jax.experimental.pallas import tpu as pltpu
from jax.sharding import PartitionSpec as P

EDGE = 4
OFFSETS = 27
LABEL_ROWS = 16
WAIT = 1_500_000_000
CHUNK = 6
BF16 = jnp.bfloat16
F32 = jnp.float32


def cube_plan():
    cell = {}
    for i in range(EDGE):
        for j in range(EDGE):
            for k in range(EDGE):
                cell[(i + 1, j + 1, k + 1)] = (i * EDGE + j) * EDGE + k
    copies = []
    free = EDGE**3
    for offset in range(OFFSETS):
        steps = (offset // 9 - 1, offset // 3 % 3 - 1, offset % 3 - 1)
        if steps == (0, 0, 0):
            continue
        ranges = [
            {-1: [(0, EDGE - 1)], 0: [(u + 1, u) for u in range(EDGE)], 1: [(EDGE + 1, 0)]}[step]
            for step in steps
        ]
        sources = []
        for x, i in ranges[0]:
            for y, j in ranges[1]:
                for z, k in ranges[2]:
                    cell[(x, y, z)] = free + len(sources)
                    sources.append((i * EDGE + j) * EDGE + k)
        at = 0
        while at < len(sources):
            count, stride = 1, 1
            if at + 1 < len(sources):
                stride = sources[at + 1] - sources[at]
                while (
                    at + count < len(sources)
                    and sources[at + count] - sources[at + count - 1] == stride
                ):
                    count += 1
            if count == 1:
                stride = 1
            copies.append((offset, sources[at], count, stride, free + at))
            at += count
        free += len(sources)
    return cell, copies, free


CELL, COPIES, CELLS = cube_plan()


def cell_runs(offset, flip):
    steps = (offset // 9, offset // 3 % 3, offset % 3)
    if flip:
        steps = tuple(2 - step for step in steps)
    runs = []
    for i in range(EDGE):
        for j in range(EDGE):
            for k in range(EDGE):
                at = CELL[(i + steps[0], j + steps[1], k + steps[2])]
                if runs and runs[-1][0] + runs[-1][1] == at:
                    runs[-1][1] += 1
                else:
                    runs.append([at, 1])
    return runs


def parity(axis, bit=0):
    return (lax.axis_index(axis) >> bit) & 1


def fill_table(table, own, sides, at=None):
    blocks = own.shape[0]
    rims = sides[0].shape[0] if at is None else sides[0].shape[1]
    tile_odd = parity("tile")
    dev_odd = parity("dev")
    firsts = (
        blocks + rims * (1 - tile_odd),
        blocks + rims * tile_odd,
        blocks + rims * (3 - dev_odd),
        blocks + rims * (2 + dev_odd),
    )
    table[0:blocks] = own[...].astype(F32)
    for first, side in zip(firsts, sides):
        table[pl.ds(first, rims)] = (side[...] if at is None else side[at]).astype(F32)
    table[blocks + 4 * rims] = jnp.zeros(table.shape[1:], F32)


def fill_cells(cells, table, near, blocks):
    voxels = table.shape[1]
    for a in range(blocks):
        cells[pl.ds(a, voxels, stride=blocks), :] = table[a]
        for offset, first, count, stride, at in COPIES:
            e = near[a, offset]
            source = pl.ds(first, count) if stride == 1 else pl.ds(first, count, stride=stride)
            if count == 1:
                cells[pl.ds(at * blocks + a, 1), :] = table[e, source, :]
            else:
                cells[pl.ds(at * blocks + a, count, stride=blocks), :] = table[e, source, :]


def fill_columns(columns, cells, blocks, flip):
    channels = cells.shape[1]
    for offset in range(OFFSETS):
        parts = [
            cells[pl.ds(at * blocks, count * blocks), :] for at, count in cell_runs(offset, flip)
        ]
        columns[:, offset * channels : (offset + 1) * channels] = jnp.concatenate(
            parts, axis=0
        ).astype(BF16)


def flipped_dot(columns, weight):
    channels = weight.shape[1]
    total = jnp.zeros((columns.shape[0], channels), F32)
    for offset in range(OFFSETS):
        part = slice(offset * channels, (offset + 1) * channels)
        total = total + lax.dot_general(
            columns[:, part], weight[part, :], (((1,), (1,)), ((), ())), preferred_element_type=F32
        )
    return total


def fetch(sems, *pairs):
    copies = [
        pltpu.make_async_copy(source, target, sems.at[n])
        for n, (source, target) in enumerate(pairs)
    ]
    for copy in copies:
        copy.start()
    return copies


def places_of(morton_pos, blocks):
    devs = [lax.div(morton_pos[r], blocks) for r in range(blocks)]
    places = []
    for r in range(blocks):
        place = jnp.int32(0)
        for earlier in range(r):
            place = place + (devs[earlier] == devs[r]).astype(jnp.int32)
        places.append(place)
    return devs, places


def pack_kernel(
    morton_hbm, rim_hbm, features_hbm, cotangent_hbm,
    outgoing, rim_rows, morton_pos, rim, features, cotangent, sems,
):
    blocks, voxels, channels = features.shape
    peers, rows, _ = outgoing.shape
    capacity = (rows - LABEL_ROWS) // voxels
    copies = fetch(
        sems, (morton_hbm, morton_pos), (features_hbm, features), (rim_hbm, rim),
        (cotangent_hbm, cotangent),
    )
    outgoing[...] = jnp.zeros(outgoing.shape, BF16)
    for p in range(peers):
        outgoing[p, capacity * voxels :, :] = jnp.full((LABEL_ROWS, channels), blocks, BF16)
    row = lax.broadcasted_iota(jnp.int32, (LABEL_ROWS, channels), 0)
    copies[0].wait()
    devs, places = places_of(morton_pos, blocks)
    copies[1].wait()
    for r in range(blocks):
        slot = morton_pos[r] - devs[r] * blocks
        place = places[r]
        outgoing[devs[r], pl.ds(pl.multiple_of(place * voxels, voxels), voxels), :] = features[r]
        held = outgoing[devs[r], capacity * voxels :, :].astype(F32)
        outgoing[devs[r], capacity * voxels :, :] = jnp.where(
            row == place, slot.astype(F32), held
        ).astype(BF16)
    copies[2].wait()
    copies[3].wait()
    for h in range(rim_rows.shape[0]):
        rim_rows[h] = cotangent[rim[h]]


def tiles_of(rows):
    return rows.astype(F32).reshape(-1, 8, rows.shape[-1])


def unpack_kernel(rim_hbm, arrived, morton, rim_rows, labels, rim, sems):
    blocks, voxels, channels = morton.shape
    copies = fetch(sems, (rim_hbm, rim))
    peers, rows, _ = arrived.shape
    capacity = (rows - LABEL_ROWS) // voxels
    held = [jnp.zeros((voxels // 8, 8, channels), F32) for _ in range(blocks)]
    for p in range(peers):
        for c in range(capacity):
            label = jnp.broadcast_to(
                arrived[p, capacity * voxels :, :].astype(F32)[c : c + 1], (8, channels)
            )
            labels[p * capacity + c] = label
            block = tiles_of(arrived[p, c * voxels : (c + 1) * voxels, :])
            for r in range(blocks):
                held[r] = jnp.where((label == r)[None], block, held[r])
    for r in range(blocks):
        morton[r] = held[r].reshape(voxels, channels).astype(BF16)
    copies[0].wait()
    for h in range(rim_rows.shape[0]):
        rim_rows[h] = morton[rim[h]]


def first_kernel(
    near_hbm, cotangent, weight, side_a, side_b, side_c, side_d,
    columns, hidden_grad, near, table, cells, sems,
):
    blocks = cotangent.shape[0]
    copies = fetch(sems, (near_hbm, near))
    fill_table(table, cotangent, (side_a, side_b, side_c, side_d))
    copies[0].wait()
    fill_cells(cells, table, near, blocks)
    fill_columns(columns, cells, blocks, True)
    hidden_grad[...] = flipped_dot(columns, weight)


def middle_kernel(
    near_hbm, rim_hbm, weight, morton, side_a, side_b, side_c, side_d,
    hidden_grad, hidden, pre_grad, rim_rows, columns, turned_hidden, turned_grad,
    near, rim, table, cells, hidden_va, pre_grad_va, sems,
):
    blocks, voxels, channels = morton.shape
    copies = fetch(sems, (near_hbm, near), (rim_hbm, rim))
    fill_table(table, morton, (side_a, side_b, side_c, side_d))
    copies[0].wait()
    fill_cells(cells, table, near, blocks)
    fill_columns(columns, cells, blocks, False)
    copies[1].wait()
    pre_one = jnp.dot(columns[...], weight[...], preferred_element_type=F32)
    gate = jax.nn.sigmoid(pre_one)
    hidden_flat = (pre_one * gate).astype(BF16)
    pre_grad_flat = (hidden_grad[...] * gate * (1.0 + pre_one * (1.0 - gate))).astype(BF16)
    hidden_va[...] = hidden_flat.astype(F32)
    pre_grad_va[...] = pre_grad_flat.astype(F32)
    for a in range(blocks):
        hidden[a] = hidden_va[pl.ds(a, voxels, stride=blocks), :].astype(BF16)
        pre_grad[a] = pre_grad_va[pl.ds(a, voxels, stride=blocks), :].astype(BF16)
    for h in range(rim_rows.shape[1]):
        rim_rows[0, h] = hidden[rim[h]]
        rim_rows[1, h] = pre_grad[rim[h]]
    turned_grad[...] = pre_grad_flat.T
    turned_hidden[...] = hidden_flat.T


def weight_sums_kernel(start, turned_hidden, turned_grad, grad_columns, columns, keep, send):
    channels = turned_grad.shape[0]
    low = jnp.full((channels, channels), parity("tile"), jnp.int32) == 0
    stop = min(start + keep.shape[0], OFFSETS)
    for offset in range(start, stop, 2):
        count = min(2, stop - offset)
        part = slice(offset * channels, (offset + count) * channels)
        two = jnp.dot(turned_hidden[...], grad_columns[:, part], preferred_element_type=F32)
        one = jnp.dot(turned_grad[...], columns[:, part], preferred_element_type=F32)
        for u in range(count):
            part = slice(u * channels, (u + 1) * channels)
            at = offset + u - start
            keep[at] = jnp.where(low, two[:, part], one[:, part].T)
            send[at] = jnp.where(low, one[:, part].T, two[:, part])
    for at in range(stop - start, keep.shape[0]):
        keep[at] = jnp.zeros(keep.shape[1:], F32)
        send[at] = jnp.zeros(send.shape[1:], F32)


def back_kernel(
    near_hbm, cotangent, weight, pre_grad, side_a, side_b, side_c, side_d, labels,
    returning, near, table, cells, columns, result, sems,
):
    blocks, voxels, channels = cotangent.shape
    peers, rows, _ = returning.shape
    capacity = rows // voxels
    copies = fetch(sems, (near_hbm, near))
    fill_table(table, pre_grad, (side_a, side_b, side_c, side_d), 1)
    copies[0].wait()
    fill_cells(cells, table, near, blocks)
    fill_columns(columns, cells, blocks, True)
    result[...] = flipped_dot(columns, weight)
    natural = [
        tiles_of(result[pl.ds(a, voxels, stride=blocks), :] + cotangent[a].astype(F32))
        for a in range(blocks)
    ]
    for p in range(peers):
        for c in range(capacity):
            label = labels[p * capacity + c]
            block = natural[0]
            for r in range(1, blocks):
                block = jnp.where((label == r)[None], natural[r], block)
            returning[p, c * voxels : (c + 1) * voxels, :] = block.reshape(
                voxels, channels
            ).astype(BF16)


def output_kernel(
    capacity, near_hbm, morton_hbm, weight, hidden, morton, side_a, side_b, side_c, side_d,
    output, flat_tiles, near, morton_pos, table, cells, columns, result, sems,
):
    blocks, voxels, channels = morton.shape
    copies = fetch(sems, (near_hbm, near), (morton_hbm, morton_pos))
    fill_table(table, hidden, (side_a, side_b, side_c, side_d), 0)
    copies[0].wait()
    fill_cells(cells, table, near, blocks)
    fill_columns(columns, cells, blocks, False)
    result[...] = jnp.dot(columns[...], weight[...], preferred_element_type=F32)
    for a in range(blocks):
        output[a] = (
            morton[a].astype(F32) + result[pl.ds(a, voxels, stride=blocks), :]
        ).astype(BF16)
    copies[1].wait()
    devs, places = places_of(morton_pos, blocks)
    for r in range(blocks):
        flat_tiles[r] = jnp.full(
            flat_tiles.shape[1:], (devs[r] * capacity + places[r]).astype(F32), F32
        )


def restore_kernel(coming_back, flat_tiles, input_grad):
    blocks, voxels, channels = input_grad.shape
    slots = coming_back.shape[0]
    held = [jnp.zeros((voxels // 8, 8, channels), F32) for _ in range(blocks)]
    for s in range(slots):
        block = tiles_of(coming_back[s])
        for r in range(blocks):
            held[r] = jnp.where((flat_tiles[r] == s)[None], block, held[r])
    for r in range(blocks):
        input_grad[r] = held[r].reshape(voxels, channels).astype(BF16)


def order_bits(group):
    x, y = parity("tile", 1), parity("dev")
    turned = (parity("tile") + group) & 1
    return jnp.where(turned == 0, x, y), jnp.where(turned == 0, y, x)


def step_bit(step, group):
    return order_bits(group)[step] if step < 2 else parity("dev", 1)


def half(rows, index):
    return pl.ds(pl.multiple_of(index * rows, rows), rows)


def split_kernel(step, group, mine, other, keep, send):
    rows = keep.shape[1]
    bit = step_bit(step, group)
    for ref, index in ((keep, bit), (send, 1 - bit)):
        at = half(rows, index)
        ref[...] = (mine[:, at, :] + other[:, at, :].astype(F32)).astype(ref.dtype)


def add_kernel(left, right, total):
    total[...] = (left[...].astype(F32) + right[...].astype(F32)).astype(total.dtype)


def join_kernel(step, group, mine, other, joined):
    rows = mine.shape[1]
    bit = step_bit(step, group)
    joined[:, half(rows, bit), :] = mine[...]
    joined[:, half(rows, 1 - bit), :] = other[...]


def write_gradient(scale, parts, grad_hbm, grad, sems):
    channels = grad.shape[1]
    copies = []
    for first in range(0, OFFSETS, CHUNK):
        last = min(first + CHUNK, OFFSETS)
        for offset in range(first, last):
            ref = parts[offset // parts[0].shape[0]]
            rows = slice(offset * channels, (offset + 1) * channels)
            grad[rows, :] = ref[offset % ref.shape[0]].astype(F32) * scale
        part = pl.ds(first * channels, (last - first) * channels)
        copies.append(
            pltpu.make_async_copy(grad.at[part], grad_hbm.at[part], sems.at[len(copies)])
        )
        copies[-1].start()
    for copy in copies:
        copy.wait()


def finish_kernel(scale, owner, *refs):
    *parts, one_hbm, two_hbm, grad, sems = refs

    @pl.when(parity("tile") == owner)
    def _():
        write_gradient(scale, parts[-2:], two_hbm, grad, sems)

    @pl.when(parity("tile") != owner)
    def _():
        write_gradient(scale, parts[-2:], one_hbm, grad, sems)


HBM = pl.BlockSpec(memory_space=pltpu.HBM)
ANY = pl.BlockSpec(memory_space=pl.ANY)
VMEM = pl.BlockSpec(memory_space=pltpu.VMEM)


def call(kernel, far, arrays, outs, scratch=(), far_outs=(), flops=0, name=None, after=(), aliases={}):
    shapes = [jax.ShapeDtypeStruct(shape, dtype) for shape, dtype in [*outs, *far_outs]]
    moved = sum(x.size * x.dtype.itemsize for x in [*far, *arrays])
    moved += sum(math.prod(s.shape) * s.dtype.itemsize for s in shapes)
    held = []
    for item in scratch:
        if isinstance(item, int):
            held.append(pltpu.SemaphoreType.DMA((item,)))
        else:
            held.append((pltpu.SMEM if item[1] == jnp.int32 else pltpu.VMEM)(*item))
    body = kernel
    if after:

        def body(*refs):
            kernel(*refs[len(after) :])

    return pl.pallas_call(
        body,
        out_shape=shapes,
        in_specs=[ANY] * len(after) + [HBM] * len(far) + [VMEM] * len(arrays),
        out_specs=[VMEM] * len(outs) + [HBM] * len(far_outs),
        scratch_shapes=held,
        input_output_aliases=aliases,
        compiler_params=pltpu.CompilerParams(vmem_limit_bytes=(63 if name == "pack" else 24) * 2**20),
        cost_estimate=pl.CostEstimate(flops=flops, bytes_accessed=moved, transcendentals=0),
        name=name,
    )(*after, *far, *arrays)


def halo(rows):
    sides = []
    for axis in ("tile", "dev"):
        count = lax.axis_size(axis)
        even = [(i, i ^ 1) for i in range(count)]
        odd = []
        for i in range(1, count - 1, 2):
            odd += [(i, i + 1), (i + 1, i)]
        sides += [lax.ppermute(rows, axis, even), lax.ppermute(rows, axis, odd)]
    return sides


def swap(rows, partner):
    tiles, devs = lax.axis_size("tile"), lax.axis_size("dev")
    pairs = []
    for t in range(tiles):
        for d in range(devs):
            other = partner(t, d)
            pairs.append((t * devs + d, other[0] * devs + other[1]))
    return lax.ppermute(rows, ("tile", "dev"), pairs)


def other_core(t, d):
    return t ^ 1, d


def partner_at(step, group):
    def partner(t, d):
        if step == 2:
            return t, d ^ 2
        along_x = ((t + group) & 1) == step
        return (t ^ 2, d) if along_x else (t, d ^ 1)

    return partner


def split_stage(step, group, mine, other, wire, after=()):
    count, rows, channels = mine.shape
    part = (count, rows // 2, channels)
    return call(
        functools.partial(split_kernel, step, group), [], [mine, other],
        [(part, F32), (part, wire)], name="split", after=after,
    )


def pair_stage(keep, send, wire, after=()):
    (mine,) = call(
        add_kernel, [], [keep, swap(send, partner_at(2, 0))], [(keep.shape, wire)],
        name="pair_sum", after=after,
    )
    return mine


def far_steps():
    rest = [(0, 1 << bit) for bit in range(2, lax.axis_size("dev").bit_length() - 1)]
    rest += [(1 << bit, 0) for bit in range(2, lax.axis_size("tile").bit_length() - 1)]
    return rest


def far_stage(mine, after=()):
    rest = far_steps()
    for step, bits in enumerate(rest):
        kind = BF16 if step == len(rest) - 1 else mine.dtype
        other = swap(mine, lambda t, d, bits=bits: (t ^ bits[0], d ^ bits[1]))
        (mine,) = call(
            add_kernel, [], [mine, other], [(mine.shape, kind)], name="far_sum", after=after
        )
        after = ()
    return mine


def join_stage(step, group, mine, after=()):
    count, rows, channels = mine.shape
    (mine,) = call(
        functools.partial(join_kernel, step, group), [], [mine, swap(mine, partner_at(step, group))],
        [((count, 2 * rows, channels), BF16)], name="join", after=after,
    )
    return mine


def finish(scale, owner, parts, held=(), after=()):
    channels = parts[0].shape[2]
    whole = ((OFFSETS * channels, channels), F32)
    first = len(after)
    return call(
        functools.partial(finish_kernel, scale, owner), held, parts, [],
        [whole, -(-OFFSETS // CHUNK)],
        [whole, whole], name="finish", after=after,
        aliases={first: 0, first + 1: 1} if held else {},
    )


def per_device(features, morton_pos, neighbours, rim, cotangent, weight_one, weight_two):
    blocks, voxels, channels = features.shape
    rims = rim.shape[0]
    peers = lax.axis_size("dev")
    tiles = lax.axis_size("tile")
    capacity = 2 * ((blocks + peers - 1) // peers)
    block = ((blocks, voxels, channels), BF16)
    rows = blocks * voxels
    depth = OFFSETS * channels
    near = ((blocks, OFFSETS), jnp.int32)
    table = ((blocks + 4 * rims + 1, voxels, channels), F32)
    cells = ((CELLS * blocks, channels), F32)
    columns = ((rows, depth), BF16)
    flat = ((rows, channels), F32)
    rim_shape = (rims, voxels, channels)
    macs = rows * depth * channels

    outgoing, cot_rim = call(
        pack_kernel, [morton_pos, rim, features, cotangent], [],
        [((peers, capacity * voxels + LABEL_ROWS, channels), BF16), (rim_shape, BF16)],
        [((blocks,), jnp.int32), ((rims,), jnp.int32), block, block, 4], flops=WAIT, name="pack",
    )
    arrived = lax.all_to_all(outgoing, "dev", split_axis=0, concat_axis=0, tiled=True)
    cot_sides = halo(cot_rim)
    grad_columns, hidden_grad = call(
        first_kernel, [neighbours], [cotangent, weight_two, *cot_sides], [columns, flat],
        [near, table, cells, 1], flops=2 * macs, name="hidden_grad",
    )
    morton, morton_rim, labels = call(
        unpack_kernel, [rim], [arrived],
        [block, (rim_shape, BF16), ((peers * capacity, 8, channels), F32)],
        [((rims,), jnp.int32), 1], flops=4 * WAIT, name="unpack",
    )
    sides = halo(morton_rim)
    hidden, pre_grad, rim_rows, morton_columns, turned_hidden, turned_grad = call(
        middle_kernel, [neighbours, rim], [weight_one, morton, *sides, hidden_grad],
        [block, block, ((2,) + rim_shape, BF16), columns, ((channels, rows), BF16),
         ((channels, rows), BF16)],
        [near, ((rims,), jnp.int32), table, cells, flat, flat, 2],
        flops=2 * macs, name="middle",
    )
    count = (OFFSETS + 1) // 2
    groups = range(2)
    wire = BF16 if len(far_steps()) == 1 else F32
    parts = [
        call(
            functools.partial(weight_sums_kernel, group * count), [],
            [turned_hidden, turned_grad, grad_columns, morton_columns],
            [((count, channels, channels), F32)] * 2, flops=2 * macs, name="weight_sums",
        )
        for group in groups
    ]
    scale = 1.0 / math.sqrt(blocks * voxels * tiles * peers)
    sides = halo(rim_rows)
    parts = [
        split_stage(0, g, parts[g][0], swap(parts[g][1], other_core), BF16)
        for g in groups
    ]
    parts = [
        split_stage(1, g, parts[g][0], swap(parts[g][1], partner_at(0, g)), BF16)
        for g in groups
    ]
    output, flat_tiles = call(
        functools.partial(output_kernel, capacity), [neighbours, morton_pos],
        [weight_two, hidden, morton, *sides], [block, ((blocks, 8, channels), F32)],
        [near, ((blocks,), jnp.int32), table, cells, columns, flat, 2], flops=2 * macs,
        name="output",
    )
    (returning,) = call(
        back_kernel, [neighbours], [cotangent, weight_one, pre_grad, *sides, labels],
        [((peers, capacity * voxels, channels), BF16)],
        [near, table, cells, columns, flat, 1], flops=2 * macs, name="back",
    )
    parts = [
        split_stage(2, g, parts[g][0], swap(parts[g][1], partner_at(1, g)), F32, after=sides[:2] if g == 1 else ())
        for g in groups
    ]
    parts = [pair_stage(*parts[g], wire, after=[returning] if g == 0 else ()) for g in groups]
    parts = [far_stage(parts[g]) for g in groups]
    coming_back = lax.all_to_all(returning, "dev", split_axis=0, concat_axis=0, tiled=True)
    parts = [join_stage(2, g, parts[g], after=[flat_tiles] if g == 0 else ()) for g in groups]
    parts = [join_stage(1, g, parts[g]) for g in groups]
    (input_grad,) = call(
        restore_kernel, [], [coming_back.reshape(peers * capacity, voxels, channels), flat_tiles],
        [block], name="restore",
    )
    parts = [join_stage(0, g, parts[g], after=[coming_back] if g == 0 else ()) for g in groups]
    others = [swap(parts[g], other_core) for g in groups]
    grads = finish(scale, 0, parts)
    grad_one, grad_two = finish(scale, 1, others, grads)
    return (output, input_grad, grad_one, grad_two)


def solution(mesh):
    placed = (
        P(("tile", "dev"), None, None),
        P(("tile", "dev")),
        P(("tile", "dev"), None),
        P(("tile", "dev")),
        P(("tile", "dev"), None, None),
        P(),
        P(),
    )
    return jax.shard_map(
        per_device,
        mesh=mesh,
        in_specs=placed,
        out_specs=(P(("tile", "dev"), None, None), P(("tile", "dev"), None, None), P(), P()),
        check_vma=False,
    )
```
